512 devices in a mesh: frame: 64 (over z, y_hi, core), head: 8 (over x, y_lo).
Axes of the slice: x: 4, y: 8 (y_hi: 4, y_lo: 2; y = y_hi * 2 + y_lo), z: 8, core: 2. Of those that a mesh axis runs over, the one named last changes fastest.
Arguments:
- q_high: bfloat16 [12288, 5120], P('frame', 'head'), may hold values from -32 to 32, as said below
- k_high: bfloat16 [12288, 5120], P('frame', 'head'), may hold values from -32 to 32
- v_high: bfloat16 [12288, 5120], P('frame', 'head'), may hold values from -6 to 6
- gain_qh: float32 [5120], P('head'), may hold values from 0.5 to 2
- gain_kh: float32 [5120], P('head'), may hold values from 0.5 to 2
- q_low: bfloat16 [12288, 5120], P(('frame', 'head')), may hold values from -32 to 32
- k_low: bfloat16 [12288, 5120], P(('frame', 'head')), may hold values from -32 to 32
- v_low: bfloat16 [12288, 5120], P(('frame', 'head')), may hold values from -6 to 6
- gain_ql: float32 [5120], replicated, may hold values from 0.5 to 2
- gain_kl: float32 [5120], replicated, may hold values from 0.5 to 2
- keyframes: int32 [2], replicated, may hold values from 0 to 63
- switch_step: int32 [1], replicated, may hold values from 10 to 30
- permutation: int32 [192], replicated, may hold values from 0 to 191, each once
Outputs:
- blended: bfloat16 [12288, 5120], P(('frame', 'head'))
The draws below stay inside these ranges and needn't reach their ends.
Inputs may be any that keep to these rules, and one draw needn't show every extreme that they name: `q_high`: each row of the query and key arrays is of order one in mean square over all channels.
All inputs are finite; a program needn't handle non-finite values.
Results may differ from the reference program's by a relative error of at most 0.012.
Values may be sent and summed in bfloat16 or wider, within the bound.
A program may use at most 64 MiB of HBM per device.

```python
import math
import jax
import jax.numpy as jnp
from jax import lax

HEADS = 40
HD = 128
TOK_F = 192
NKEY = 2
STEPS = 40
FRAMES = 64
TOKENS = 12288
C = 5120


def draw_q_high(key, part):
    key = jax.random.fold_in(key, 11)
    own = jax.random.normal(key, (TOKENS, HEADS * HD), jnp.float32)
    return own.astype(jnp.bfloat16)


def draw_k_high(key, part):
    key = jax.random.fold_in(key, 12)
    own = jax.random.normal(key, (TOKENS, HEADS * HD), jnp.float32)
    return own.astype(jnp.bfloat16)


def draw_q_low(key, part):
    key = jax.random.fold_in(key, 13)
    own = jax.random.normal(key, (TOKENS, HEADS * HD), jnp.float32)
    return own.astype(jnp.bfloat16)


def draw_k_low(key, part):
    key = jax.random.fold_in(key, 14)
    own = jax.random.normal(key, (TOKENS, HEADS * HD), jnp.float32)
    return own.astype(jnp.bfloat16)


def block_scale(rng, extent, shards, low, high):
    level = 1.0
    for dim, shards_of in shards:
        draws = jax.random.uniform(jax.random.fold_in(jax.random.fold_in(rng, 6), dim), (shards_of,), jnp.float32, low / len(shards), high / len(shards))
        level = level * jnp.repeat(jnp.exp(draws), extent[dim] // shards_of).reshape((-1,) + (1,) * (len(extent) - 1 - dim))
    return level


def noise(own_key, shape, deviation, limit, cuts=(), kind=jnp.bfloat16):
    values = deviation * jax.random.normal(own_key, shape, jnp.float32)
    if cuts:
        values = values * block_scale(own_key, shape, cuts, -0.22, 0.18)
    return jnp.clip(values, -limit, limit).astype(kind)


def setup_inputs(seed: int = 0) -> dict:
    key_of = jax.random.split(jax.random.key(seed), 14)
    return {
        "q_high": draw_q_high(jax.random.fold_in(key_of[13], 71), 0),
        "k_high": draw_k_high(jax.random.fold_in(key_of[13], 71), 0),
        "v_high": noise(key_of[2], (TOKENS, C), 1.0, 6.0, ((0, 64), (1, 8))),
        "gain_qh": jnp.clip(jnp.exp(math.log(2.0) - 1.3862944 * jax.random.uniform(key_of[3], (C,), jnp.float32) ** block_scale(key_of[3], (C,), ((0, 8),), -0.2, 0.2)), 0.5, 2.0),
        "gain_kh": jnp.clip(jnp.exp(math.log(2.0) - 1.3862944 * jax.random.uniform(key_of[4], (C,), jnp.float32) ** block_scale(key_of[4], (C,), ((0, 8),), -0.2, 0.2)), 0.5, 2.0),
        "q_low": draw_q_low(jax.random.fold_in(key_of[13], 71), 0),
        "k_low": draw_k_low(jax.random.fold_in(key_of[13], 71), 0),
        "v_low": noise(key_of[7], (TOKENS, C), 1.0, 6.0, ((0, 512),)),
        "gain_ql": jnp.clip(jnp.exp(jax.random.uniform(key_of[8], (C,), jnp.float32, math.log(0.5), math.log(2.0))), 0.5, 2.0),
        "gain_kl": jnp.clip(jnp.exp(jax.random.uniform(key_of[9], (C,), jnp.float32, math.log(0.5), math.log(2.0))), 0.5, 2.0),
        "keyframes": jax.random.randint(key_of[10], (NKEY,), 0, FRAMES).astype(jnp.int32),
        "switch_step": jax.random.randint(key_of[11], (1,), STEPS // 4, 3 * STEPS // 4 + 1).astype(jnp.int32),
        "permutation": jax.random.permutation(key_of[12], TOK_F).astype(jnp.int32),
    }


def norm_rows(values, gain):
    floats = values.astype(jnp.float32)
    scale = lax.rsqrt(lax.optimization_barrier(jnp.mean(floats * floats, axis=-1, keepdims=True)) + 1e-06)
    return (floats * scale * gain).astype(jnp.bfloat16)

def attend(query, keys, values):
    rows = query.shape[0]
    qheads = query.reshape(rows, HEADS, HD).transpose(1, 0, 2)
    kheads = keys.reshape(keys.shape[0], HEADS, HD).transpose(1, 0, 2)
    vheads = values.reshape(values.shape[0], HEADS, HD).transpose(1, 0, 2)

    def one_head(items):
        qpart, kpart, vpart = items
        scores = jnp.einsum('qd,kd->qk', qpart.astype(jnp.float32), kpart.astype(jnp.float32)) * HD ** (-0.5)
        top = lax.optimization_barrier(jnp.max(scores, axis=-1, keepdims=True))
        expo = jnp.exp(scores - top)
        weights = (expo / lax.optimization_barrier(jnp.sum(expo, axis=-1, keepdims=True))).astype(jnp.bfloat16)
        return jnp.einsum('qk,kd->qd', weights.astype(jnp.float32), vpart.astype(jnp.float32)).astype(jnp.bfloat16)
    outputs = lax.map(one_head, (qheads, kheads, vheads))
    return outputs.transpose(1, 0, 2).reshape(rows, HEADS * HD)

def frame_attention(query, keys, values, keyframes):
    width = HEADS * HD
    qframes = query.reshape(FRAMES, TOK_F, width)
    kframes = keys.reshape(FRAMES, TOK_F, width)
    vframes = values.reshape(FRAMES, TOK_F, width)
    key_rows = kframes[keyframes].reshape(NKEY * TOK_F, width)
    value_rows = vframes[keyframes].reshape(NKEY * TOK_F, width)

    def per_frame(index):
        keys_all = jnp.concatenate([kframes[index], key_rows], axis=0)
        values_all = jnp.concatenate([vframes[index], value_rows], axis=0)
        return attend(qframes[index], keys_all, values_all)
    return lax.map(per_frame, jnp.arange(FRAMES, dtype=jnp.int32))

def reference(q_high, k_high, v_high, gain_qh, gain_kh, q_low, k_low, v_low, gain_ql, gain_kl, keyframes, switch_step, permutation):
    o_high = frame_attention(norm_rows(q_high, gain_qh), norm_rows(k_high, gain_kh), v_high, keyframes)
    o_low = frame_attention(norm_rows(q_low, gain_ql), norm_rows(k_low, gain_kl), v_low, keyframes)
    moved = o_high[:, permutation, :]
    lam = switch_step[0].astype(jnp.float32) / STEPS
    mixed = (1.0 - lam) * moved.astype(jnp.float32) + lam * o_low.astype(jnp.float32)
    return mixed.astype(jnp.bfloat16).reshape(TOKENS, HEADS * HD)
```

```python
import functools
import math

import jax
import jax.numpy as jnp
from jax import lax
from jax.experimental import pallas as pl
from jax.experimental.pallas import tpu as pltpu
from jax.sharding import PartitionSpec as P

HEADS = 40
HD = 128
STEPS = 40
EPS = 1e-06
TOK = 192
W = 640
WIDTH = HEADS * HD
LOCAL = 24
BF = jnp.bfloat16
F32 = jnp.float32
MESH = pl.DeviceIdType.MESH
QSCALE = HD ** (-0.5) * math.log2(math.e)


def kernel(
    kf,
    step_ref,
    q_high,
    k_high,
    v_high,
    gain_qh,
    gain_kh,
    q_low,
    k_low,
    v_low,
    gain_ql,
    gain_kl,
    perm,
    out,
    KV,
    Q,
    OH,
    CH,
    H1R,
    RZ,
    ZC,
    RY,
    SKV,
    RKV,
    SQ,
    RQ,
    SS,
    RS,
    MB,
    RB,
    send_sems,
    sum_sems,
    akv_sems,
    aq_sems,
    back_sems,
    h1_sems,
    rz_sems,
    ry_sems,
    yg_sems,
    ag_sems,
    sb_sems,
):
    f = lax.axis_index("frame")
    h = lax.axis_index("head")
    z = f // 8
    y = (f // 2) % 4
    c = f % 2
    sgn = (1 - 2 * c, 2 * c - 1)

    def at(zz, yy, cc, hh):
        return {"frame": (zz * 4 + yy) * 2 + cc, "head": hh}

    sibling = at(z, y, 1 - c, h)
    zdev = [at((z + s + 8) % 8, y, c, h) for s in sgn]
    ydev = [at(z, (y + j) % 4, c, h) for j in range(4)]
    hidx = [(h + j) % 8 for j in range(8)]
    hdev = [at(z, y, c, hidx[j]) for j in range(8)]

    barrier = pltpu.get_barrier_semaphore()
    partners = [sibling] + zdev + ydev[1:] + hdev[1:]
    for dev in partners:
        pl.semaphore_signal(barrier, inc=1, device_id=dev, device_id_type=MESH)

    count = [0]
    ends = []

    def rcopy(src, dst, rsem, dev, cond=None):
        index = count[0]
        count[0] += 1
        copy = pltpu.make_async_remote_copy(
            src_ref=src,
            dst_ref=dst,
            send_sem=send_sems.at[index],
            recv_sem=rsem,
            device_id=dev,
            device_id_type=MESH,
        )
        if cond is None:
            copy.start()
        else:
            pl.when(cond)(copy.start)
        ends.append((copy, cond))

    def arrived(dst, rsem):
        pltpu.make_async_remote_copy(
            src_ref=dst,
            dst_ref=dst,
            send_sem=send_sems.at[0],
            recv_sem=rsem,
            device_id=sibling,
            device_id_type=MESH,
        ).wait_recv()

    def rows_sum(ref):
        x = ref[...].astype(F32)
        x = x * x
        hi = x.astype(BF)
        lo = (x - hi.astype(F32)).astype(BF)
        ones = jnp.ones((8, W), BF)
        dims = (((1,), (1,)), ((), ()))
        return lax.dot_general(ones, hi, dims, preferred_element_type=F32) + lax.dot_general(
            ones, lo, dims, preferred_element_type=F32
        )

    eight = lax.broadcasted_iota(jnp.int32, (8, TOK), 0)
    SS[...] = jnp.where(eight < 4, rows_sum(q_high), rows_sum(k_high))
    RS[h] = SS[...]
    KV[0, 1, 0:TOK] = v_high[...]

    pl.semaphore_wait(barrier, len(partners))

    for j in range(1, 8):
        rcopy(SS, RS.at[h], sum_sems.at[h], hdev[j])

    def h1_rows(rh, core):
        return pl.ds(pl.multiple_of(96 * rh + 48 * core, 16), 48)

    def h1_send(e, kv):
        for rh in range(2):
            rcopy(
                KV.at[e, kv, h1_rows(rh, 1 - c)],
                H1R.at[e, kv, rh],
                h1_sems.at[e, kv, rh],
                sibling,
            )

    h1_send(0, 1)

    def factor(ref):
        x = ref[...].astype(F32)
        return lax.rsqrt(jnp.sum(x * x, axis=1, keepdims=True) / WIDTH + EPS)

    fk = factor(k_low)
    for p in range(8):
        cols = slice(W * p, W * p + W)
        kn = k_low[:, cols].astype(F32) * fk * gain_kl[:, cols]
        SKV[p] = jnp.concatenate([kn, v_low[:, cols].astype(F32)], axis=0).astype(BF)
    RKV[h] = SKV[h]
    for j in range(1, 8):
        rcopy(SKV.at[hidx[j]], RKV.at[h], akv_sems.at[h], hdev[j])
    fq = factor(q_low)
    for p in range(8):
        cols = slice(W * p, W * p + W)
        qn = q_low[:, cols].astype(F32) * (fq * QSCALE) * gain_ql[:, cols]
        SQ[p] = jnp.concatenate([qn, jnp.zeros((8, W), F32)], axis=0).astype(BF)
    RQ[h] = SQ[h]
    for j in range(1, 8):
        rcopy(SQ.at[hidx[j]], RQ.at[h], aq_sems.at[h], hdev[j])

    for j in range(1, 8):
        arrived(RS.at[hidx[j]], sum_sems.at[hidx[j]])
    total = RS[0]
    for p in range(1, 8):
        total = total + RS[p]
    total = lax.rsqrt(total / WIDTH + EPS)

    def spread_rows(row):
        pick = jnp.where(lax.broadcasted_iota(jnp.int32, (8, HD), 0) == row, 1.0, 0.0)
        return lax.dot_general(
            total,
            pick,
            (((0,), (0,)), ((), ())),
            precision=lax.Precision.HIGHEST,
            preferred_element_type=F32,
        )

    kfac = spread_rows(4)
    for g in range(5):
        cols = slice(HD * g, HD * g + HD)
        KV[0, 0, 0:TOK, cols] = (k_high[:, cols].astype(F32) * kfac * gain_kh[:, cols]).astype(BF)
    h1_send(0, 0)
    qfac = spread_rows(0) * QSCALE
    hot = jnp.where(lax.broadcasted_iota(jnp.int32, (TOK, TOK), 0) == perm[...], 1.0, 0.0).astype(BF)
    for g in range(5):
        cols = slice(HD * g, HD * g + HD)
        qn = (q_high[:, cols].astype(F32) * qfac * gain_qh[:, cols]).astype(BF)
        Q[0, :, cols] = lax.dot_general(
            hot, qn, (((0,), (0,)), ((), ())), preferred_element_type=F32
        ).astype(BF)

    def place(e, o, k, n=1):
        row = TOK + TOK * (o // 4) + 96 * (o % 2) + 48 * c + 16 * k
        return KV.at[e, (o // 2) % 2, pl.ds(pl.multiple_of(row, 16), 16 * n)]

    def chunk(k):
        return pl.ds(16 * k, 16)

    far = ((0, 2), (1,))

    def gather_pair(e):
        for kv in range(2):
            for rh in range(2):
                arrived(H1R.at[e, kv, rh], h1_sems.at[e, kv, rh])
                mine = KV[e, kv, h1_rows(rh, c)]
                other = H1R[e, kv, rh]
                for s in range(2):
                    CH[e, s * 4 + kv * 2 + rh] = jnp.where(kf[s] % 2 == c, mine, other)

    def slot_of(o):
        return jnp.where(o // 4 == 0, kf[0], kf[1])

    def rs_send(e, t):
        for k in (0, 2, 1):
            for d in range(2):
                o = (z + sgn[d] * (5 - t) + 8) % 8
                if t == 1 and k not in far[d]:
                    continue
                if t == 1 or (t == 2 and k not in far[d]):
                    src = CH.at[e, o, chunk(k)]
                else:
                    got = RZ.at[e, d, t - 2, chunk(k)]
                    arrived(got, rz_sems.at[e, d, t - 2, k])
                    got[...] = jnp.where(slot_of(o) // 8 == z, CH[e, o, chunk(k)], got[...])
                    src = got
                rcopy(src, RZ.at[e, d, t - 1, chunk(k)], rz_sems.at[e, d, t - 1, k], zdev[d])

    def yowner(k):
        return (k + z + 2 * c) % 4

    def y_send(e):
        root = slot_of(z) // 8
        away = ((z - root) * sgn[0] + 8) % 8
        for k in range(3):
            for d in range(2):
                arrived(RZ.at[e, d, 3, chunk(k)], rz_sems.at[e, d, 3, k])
            limit = 5 if k in far[0] else 4
            mixed = jnp.where(away < limit, RZ[e, 0, 3, chunk(k)], RZ[e, 1, 3, chunk(k)])
            ZC[e, k] = jnp.where(away == 0, CH[e, z, chunk(k)], mixed)
            yo = yowner(k)
            rcopy(
                ZC.at[e, k], RY.at[e, y], ry_sems.at[e, y], at(z, yo, c, h), cond=yo != y
            )

    def y_own(e):
        kme = (y - z - 2 * c + 12) % 4
        own = kme < 3
        kme = jnp.minimum(kme, 2)

        @pl.when(own)
        def _():
            for j in range(1, 4):
                yy = (y + j) % 4
                arrived(RY.at[e, yy], ry_sems.at[e, yy])
            RY[e, y] = ZC[e, kme]
            root = (slot_of(z) // 2) % 4
            value = RY[e, 0]
            for yy in range(1, 4):
                value = jnp.where(root == yy, RY[e, yy], value)
            place(e, z, kme)[...] = value

        for j in range(1, 4):
            rcopy(place(e, z, kme), place(e, z, kme), yg_sems.at[e, kme], ydev[j], cond=own)

    def ag_send(e, j):
        for k in (0, 2, 1):
            if j == 1:

                @pl.when(yowner(k) != y)
                def _():
                    arrived(place(e, z, k), yg_sems.at[e, k])

            for d in range(2):
                o = (z - sgn[d] * (j - 1) + 8) % 8
                if j > 1:
                    arrived(place(e, o, k), ag_sems.at[e, d, j - 2, k])
                if j == 4 and k not in far[d]:
                    continue
                rcopy(place(e, o, k), place(e, o, k), ag_sems.at[e, d, j - 1, k], zdev[d])
        for d in range(2 if j > 1 else 1):
            o = (z - sgn[d] * (j - 1) + 8) % 8
            i = 2 * (j - 1) + d - (1 if j > 1 else 0)
            rcopy(place(e, o, 0, 3), place(e, o, 0, 3), sb_sems.at[e, i], sibling)

    def ag_last(e):
        o = (z + 4) % 8
        for d in range(2):
            for k in far[d]:
                arrived(place(e, o, k), ag_sems.at[e, d, 3, k])
                rcopy(place(e, o, k), place(e, o, k), sb_sems.at[e, 7 + k], sibling)

    def sib_place(e, o, k, n=1):
        row = TOK + TOK * (o // 4) + 96 * (o % 2) + 48 * (1 - c) + 16 * k
        return KV.at[e, (o // 2) % 2, pl.ds(pl.multiple_of(row, 16), 16 * n)]

    def sib_wait(e):
        sib_sgn = (sgn[1], sgn[0])
        for j in range(1, 5):
            for d in range(2 if j > 1 else 1):
                o = (z - sib_sgn[d] * (j - 1) + 8) % 8
                i = 2 * (j - 1) + d - (1 if j > 1 else 0)
                arrived(sib_place(e, o, 0, 3), sb_sems.at[e, i])
        o = (z + 4) % 8
        for k in range(3):
            arrived(sib_place(e, o, k), sb_sems.at[e, 7 + k])

    lam = step_ref[0].astype(F32) / STEPS

    def heads(e):
        def one(g, carry):
            cols = pl.ds(pl.multiple_of(g * HD, HD), HD)
            q = Q[e, :, cols]
            keys = KV[e, 0, :, cols]
            vals = KV[e, 1, :, cols]
            s = lax.dot_general(q, keys, (((1,), (1,)), ((), ())), preferred_element_type=F32)
            p = jnp.exp2(s - jnp.max(s, axis=1, keepdims=True)).astype(BF)
            both = jnp.concatenate([vals, jnp.ones((3 * TOK, HD), BF)], axis=1)
            o = lax.dot_general(p, both, (((1,), (0,)), ((), ())), preferred_element_type=F32)
            o = (o[:, :HD] / o[:, HD:]).astype(BF)
            if e == 0:
                OH[:, cols] = o
            else:
                mixed = (1.0 - lam) * OH[:, cols].astype(F32) + lam * o.astype(F32)
                pad = jnp.zeros((8, HD), F32)
                for p8 in range(8):
                    rows = mixed[LOCAL * p8 : LOCAL * p8 + LOCAL]
                    MB[p8, :, cols] = jnp.concatenate([rows, pad], axis=0).astype(BF)
            return carry

        lax.fori_loop(0, 5, one, 0)

    def low_keys():
        for j in range(1, 8):
            arrived(RKV.at[hidx[j]], akv_sems.at[hidx[j]])
        for p in range(4):
            a = RKV[2 * p].astype(F32)
            b = RKV[2 * p + 1].astype(F32)
            rows = slice(48 * p, 48 * p + 48)
            KV[1, 0, rows] = jnp.concatenate([a[:LOCAL], b[:LOCAL]], axis=0).astype(BF)
            KV[1, 1, rows] = jnp.concatenate([a[LOCAL:], b[LOCAL:]], axis=0).astype(BF)

    def low_queries():
        for j in range(1, 8):
            arrived(RQ.at[hidx[j]], aq_sems.at[hidx[j]])
        for p in range(4):
            a = RQ[2 * p].astype(F32)
            b = RQ[2 * p + 1].astype(F32)
            Q[1, 48 * p : 48 * p + 48] = jnp.concatenate([a[:LOCAL], b[:LOCAL]], axis=0).astype(BF)

    gather_pair(0)
    rs_send(0, 1)
    rs_send(0, 2)
    rs_send(0, 3)
    low_keys()
    h1_send(1, 0)
    h1_send(1, 1)
    rs_send(0, 4)
    gather_pair(1)
    rs_send(1, 1)
    y_send(0)
    rs_send(1, 2)
    y_own(0)
    rs_send(1, 3)
    ag_send(0, 1)
    rs_send(1, 4)
    ag_send(0, 2)
    y_send(1)
    ag_send(0, 3)
    y_own(1)
    ag_send(0, 4)
    ag_send(1, 1)
    ag_last(0)
    low_queries()
    ag_send(1, 2)
    sib_wait(0)
    ag_send(1, 3)
    ag_send(1, 4)
    heads(0)
    ag_last(1)
    sib_wait(1)
    heads(1)

    RB[h] = MB[h]
    for j in range(1, 8):
        rcopy(MB.at[hidx[j]], RB.at[h], back_sems.at[h], hdev[j])
    for j in range(1, 8):
        arrived(RB.at[hidx[j]], back_sems.at[hidx[j]])
    for p in range(8):
        out[:, W * p : W * p + W] = RB[p, 0:LOCAL]

    for copy, cond in ends:
        if cond is None:
            copy.wait_send()
        else:
            pl.when(cond)(copy.wait_send)


def body(
    q_high,
    k_high,
    v_high,
    gain_qh,
    gain_kh,
    q_low,
    k_low,
    v_low,
    gain_ql,
    gain_kl,
    keyframes,
    switch_step,
    permutation,
):
    smem = pl.BlockSpec(memory_space=pltpu.SMEM)
    vmem = pl.BlockSpec(memory_space=pltpu.VMEM)
    dma = pltpu.SemaphoreType.DMA
    return pl.pallas_call(
        kernel,
        out_shape=jax.ShapeDtypeStruct((LOCAL, WIDTH), BF),
        in_specs=[smem, smem] + [vmem] * 11,
        out_specs=vmem,
        scratch_shapes=[
            pltpu.VMEM((2, 2, 3 * TOK, W), BF),
            pltpu.VMEM((2, TOK, W), BF),
            pltpu.VMEM((TOK, W), BF),
            pltpu.VMEM((2, 8, 48, W), BF),
            pltpu.VMEM((2, 2, 2, 48, W), BF),
            pltpu.VMEM((2, 2, 4, 48, W), BF),
            pltpu.VMEM((2, 3, 16, W), BF),
            pltpu.VMEM((2, 4, 16, W), BF),
            pltpu.VMEM((8, 48, W), BF),
            pltpu.VMEM((8, 48, W), BF),
            pltpu.VMEM((8, 32, W), BF),
            pltpu.VMEM((8, 32, W), BF),
            pltpu.VMEM((8, TOK), F32),
            pltpu.VMEM((8, 8, TOK), F32),
            pltpu.VMEM((8, 32, W), BF),
            pltpu.VMEM((8, 32, W), BF),
            dma((200,)),
            dma((8,)),
            dma((8,)),
            dma((8,)),
            dma((8,)),
            dma((2, 2, 2)),
            dma((2, 2, 4, 3)),
            dma((2, 4)),
            dma((2, 4)),
            dma((2, 2, 4, 3)),
            dma((2, 10)),
        ],
        compiler_params=pltpu.CompilerParams(
            collective_id=0, has_side_effects=True, vmem_limit_bytes=40 * 1024 * 1024
        ),
    )(
        keyframes,
        switch_step,
        q_high,
        k_high,
        v_high,
        gain_qh.reshape(1, W),
        gain_kh.reshape(1, W),
        q_low,
        k_low,
        v_low,
        gain_ql.reshape(1, WIDTH),
        gain_kl.reshape(1, WIDTH),
        permutation.reshape(1, TOK),
    )


def solution(mesh):
    return jax.shard_map(
        body,
        mesh=mesh,
        in_specs=(
            P("frame", "head"),
            P("frame", "head"),
            P("frame", "head"),
            P("head"),
            P("head"),
            P(("frame", "head"), None),
            P(("frame", "head"), None),
            P(("frame", "head"), None),
            P(),
            P(),
            P(),
            P(),
            P(),
        ),
        out_specs=P(("frame", "head"), None),
        check_vma=False,
    )
```

```python
import functools
import math

import jax
import jax.numpy as jnp
from jax import lax
from jax.experimental import pallas as pl
from jax.experimental.pallas import tpu as pltpu
from jax.sharding import PartitionSpec as P

HEADS = 40
HD = 128
STEPS = 40
EPS = 1e-06
TOK = 192
W = 640
WIDTH = HEADS * HD
LOCAL = 24
BF = jnp.bfloat16
F32 = jnp.float32
MESH = pl.DeviceIdType.MESH
QSCALE = HD ** (-0.5) * math.log2(math.e)


def kernel(
    kf,
    step_ref,
    q_high_hbm,
    k_high_hbm,
    v_high_hbm,
    gain_qh_hbm,
    gain_kh_hbm,
    q_low_hbm,
    k_low_hbm,
    v_low_hbm,
    gain_ql_hbm,
    gain_kl_hbm,
    perm_hbm,
    out,
    q_high,
    k_high,
    q_low,
    k_low,
    v_low,
    gain_qh,
    gain_kh,
    gain_ql,
    gain_kl,
    perm,
    KV,
    Q,
    OH,
    CH,
    H1R,
    RZ,
    ZC,
    RY,
    SKV,
    RKV,
    SQ,
    RQ,
    SS,
    RS,
    MB,
    RB,
    load_sems,
    send_sems,
    sum_sems,
    akv_sems,
    aq_sems,
    back_sems,
    h1_sems,
    rz_sems,
    ry_sems,
    yg_sems,
    ag_sems,
    sb_sems,
):
    f = lax.axis_index("frame")
    h = lax.axis_index("head")
    z = f // 8
    y = (f // 2) % 4
    c = f % 2
    sgn = (1 - 2 * c, 2 * c - 1)

    def at(zz, yy, cc, hh):
        return {"frame": (zz * 4 + yy) * 2 + cc, "head": hh}

    sibling = at(z, y, 1 - c, h)
    zdev = [at((z + s + 8) % 8, y, c, h) for s in sgn]
    zdev2 = [at((z + 2 * s + 8) % 8, y, c, h) for s in sgn]
    ydev = [at(z, (y + j) % 4, c, h) for j in range(4)]
    hidx = [(h + j) % 8 for j in range(8)]
    hdev = [at(z, y, c, hidx[j]) for j in range(8)]

    loads = []
    for src, dst in (
        (k_high_hbm, k_high),
        (q_high_hbm, q_high),
        (v_high_hbm, KV.at[0, 1, pl.ds(0, TOK)]),
        (k_low_hbm, k_low),
        (v_low_hbm, v_low),
        (gain_kl_hbm, gain_kl),
        (q_low_hbm, q_low),
        (gain_ql_hbm, gain_ql),
        (gain_kh_hbm, gain_kh),
        (gain_qh_hbm, gain_qh),
        (perm_hbm, perm),
    ):
        loads.append(pltpu.make_async_copy(src, dst, load_sems.at[len(loads)]))
        loads[-1].start()

    barrier = pltpu.get_barrier_semaphore()
    partners = [sibling] + zdev + zdev2 + ydev[1:] + hdev[1:]
    for dev in partners:
        pl.semaphore_signal(barrier, inc=1, device_id=dev, device_id_type=MESH)

    count = [0]
    ends = []

    def rcopy(src, dst, rsem, dev, cond=None):
        index = count[0]
        count[0] += 1
        copy = pltpu.make_async_remote_copy(
            src_ref=src,
            dst_ref=dst,
            send_sem=send_sems.at[index],
            recv_sem=rsem,
            device_id=dev,
            device_id_type=MESH,
        )
        if cond is None:
            copy.start()
        else:
            pl.when(cond)(copy.start)
        ends.append((copy, cond))

    def arrived(dst, rsem):
        pltpu.make_async_remote_copy(
            src_ref=dst,
            dst_ref=dst,
            send_sem=send_sems.at[0],
            recv_sem=rsem,
            device_id=sibling,
            device_id_type=MESH,
        ).wait_recv()

    def rows_sum(ref):
        x = ref[...].astype(F32)
        x = x * x
        hi = x.astype(BF)
        lo = (x - hi.astype(F32)).astype(BF)
        ones = jnp.ones((8, W), BF)
        dims = (((1,), (1,)), ((), ()))
        return lax.dot_general(ones, hi, dims, preferred_element_type=F32) + lax.dot_general(
            ones, lo, dims, preferred_element_type=F32
        )

    loads[0].wait()
    loads[1].wait()
    eight = lax.broadcasted_iota(jnp.int32, (8, TOK), 0)
    SS[...] = jnp.where(eight < 4, rows_sum(q_high), rows_sum(k_high))
    RS[h] = SS[...]
    loads[2].wait()

    pl.semaphore_wait(barrier, len(partners))

    for j in range(1, 8):
        rcopy(SS, RS.at[h], sum_sems.at[h], hdev[j])

    def h1_rows(rh, core):
        return pl.ds(pl.multiple_of(96 * rh + 48 * core, 16), 48)

    def h1_send(e, kv):
        for rh in range(2):
            rcopy(
                KV.at[e, kv, h1_rows(rh, 1 - c)],
                H1R.at[e, kv, rh],
                h1_sems.at[e, kv, rh],
                sibling,
            )

    h1_send(0, 1)

    def factor(ref):
        x = ref[...].astype(F32)
        return lax.rsqrt(jnp.sum(x * x, axis=1, keepdims=True) / WIDTH + EPS)

    for i in (3, 4, 5):
        loads[i].wait()
    fk = factor(k_low)
    for p in range(8):
        cols = slice(W * p, W * p + W)
        kn = k_low[:, cols].astype(F32) * fk * gain_kl[cols].reshape(1, W)
        SKV[p] = jnp.concatenate([kn, v_low[:, cols].astype(F32)], axis=0).astype(BF)
    RKV[h] = SKV[h]
    for j in range(1, 8):
        rcopy(SKV.at[hidx[j]], RKV.at[h], akv_sems.at[h], hdev[j])
    loads[6].wait()
    loads[7].wait()
    fq = factor(q_low)
    for p in range(8):
        cols = slice(W * p, W * p + W)
        qn = q_low[:, cols].astype(F32) * (fq * QSCALE) * gain_ql[cols].reshape(1, W)
        SQ[p] = jnp.concatenate([qn, jnp.zeros((8, W), F32)], axis=0).astype(BF)
    RQ[h] = SQ[h]
    for j in range(1, 8):
        rcopy(SQ.at[hidx[j]], RQ.at[h], aq_sems.at[h], hdev[j])

    for j in range(1, 8):
        arrived(RS.at[hidx[j]], sum_sems.at[hidx[j]])
    total = RS[0]
    for p in range(1, 8):
        total = total + RS[p]
    total = lax.rsqrt(total / WIDTH + EPS)

    def spread_rows(row):
        pick = jnp.where(lax.broadcasted_iota(jnp.int32, (8, HD), 0) == row, 1.0, 0.0)
        return lax.dot_general(
            total,
            pick,
            (((0,), (0,)), ((), ())),
            precision=lax.Precision.HIGHEST,
            preferred_element_type=F32,
        )

    for i in (8, 9, 10):
        loads[i].wait()
    kfac = spread_rows(4)
    for g in range(5):
        cols = slice(HD * g, HD * g + HD)
        KV[0, 0, 0:TOK, cols] = (k_high[:, cols].astype(F32) * kfac * gain_kh[cols].reshape(1, HD)).astype(BF)
    h1_send(0, 0)
    qfac = spread_rows(0) * QSCALE
    hot = jnp.where(lax.broadcasted_iota(jnp.int32, (TOK, TOK), 0) == perm[...].reshape(1, TOK), 1.0, 0.0).astype(BF)
    for g in range(5):
        cols = slice(HD * g, HD * g + HD)
        qn = (q_high[:, cols].astype(F32) * qfac * gain_qh[cols].reshape(1, HD)).astype(BF)
        Q[0, :, cols] = lax.dot_general(
            hot, qn, (((0,), (0,)), ((), ())), preferred_element_type=F32
        ).astype(BF)

    def place(e, o, k, n=1):
        row = TOK + TOK * (o // 4) + 96 * (o % 2) + 48 * c + 16 * k
        return KV.at[e, (o // 2) % 2, pl.ds(pl.multiple_of(row, 16), 16 * n)]

    def chunk(k, n=1):
        return pl.ds(16 * k, 16 * n)

    far = ((0, 2), (2, 1))

    def gather_pair(e):
        for kv in range(2):
            for rh in range(2):
                arrived(H1R.at[e, kv, rh], h1_sems.at[e, kv, rh])
                mine = KV[e, kv, h1_rows(rh, c)]
                other = H1R[e, kv, rh]
                for s in range(2):
                    CH[e, s * 4 + kv * 2 + rh] = jnp.where(kf[s] % 2 == c, mine, other)

    def slot_of(o):
        return jnp.where(o // 4 == 0, kf[0], kf[1])

    def rs_first(e):
        for d in range(2):
            k, n = far[d]
            o3, o4, o1 = ((z + i * sgn[d] + 8) % 8 for i in (3, 4, 1))
            rcopy(CH.at[e, o3], RZ.at[e, d, 0], rz_sems.at[e, d, 0], zdev[d])
            rcopy(CH.at[e, o4, chunk(k, n)], RZ.at[e, d, 1, chunk(k, n)], rz_sems.at[e, d, 1], zdev2[d])
        for d in range(2):
            o1 = (z + sgn[d] + 8) % 8
            rcopy(CH.at[e, o1], RZ.at[e, d, 2], rz_sems.at[e, d, 2], zdev[d])

    def rs_second(e):
        for d in range(2):
            k, n = far[d]
            o2 = (z + 2 * sgn[d] + 8) % 8
            away = ((z - slot_of(o2) // 8) * sgn[d] + 8) % 8
            arrived(RZ.at[e, d, 0], rz_sems.at[e, d, 0])
            arrived(RZ.at[e, d, 1, chunk(k, n)], rz_sems.at[e, d, 1])
            RZ[e, d, 0] = jnp.where(away == 0, CH[e, o2], RZ[e, d, 0])
            RZ[e, d, 0, chunk(k, n)] = jnp.where(
                away == 2, RZ[e, d, 1, chunk(k, n)], RZ[e, d, 0, chunk(k, n)]
            )
            rcopy(RZ.at[e, d, 0], RZ.at[e, d, 3], rz_sems.at[e, d, 3], zdev2[d])

    def yowner(k):
        return (k + 2 * c) % 4

    def y_send(e):
        root = slot_of(z) // 8
        away = ((z - root) * sgn[0] + 8) % 8
        for d in range(2):
            arrived(RZ.at[e, d, 2], rz_sems.at[e, d, 2])
        for d in range(2):
            arrived(RZ.at[e, d, 3], rz_sems.at[e, d, 3])
        for k in range(3):
            limit = 5 if k < far[0][1] else 4
            value = jnp.where(away == 1, RZ[e, 0, 2, chunk(k)], RZ[e, 0, 3, chunk(k)])
            value = jnp.where(away >= limit, RZ[e, 1, 3, chunk(k)], value)
            value = jnp.where(away == 7, RZ[e, 1, 2, chunk(k)], value)
            ZC[e, k] = jnp.where(away == 0, CH[e, z, chunk(k)], value)
            yo = yowner(k)
            rcopy(
                ZC.at[e, k], RY.at[e, y], ry_sems.at[e, y], at(z, yo, c, h), cond=yo != y
            )

    def y_own(e):
        kme = (y - 2 * c + 4) % 4
        own = kme < 3
        kme = jnp.minimum(kme, 2)

        @pl.when(own)
        def _():
            for j in range(1, 4):
                yy = (y + j) % 4
                arrived(RY.at[e, yy], ry_sems.at[e, yy])
            RY[e, y] = ZC[e, kme]
            root = (slot_of(z) // 2) % 4
            value = RY[e, 0]
            for yy in range(1, 4):
                value = jnp.where(root == yy, RY[e, yy], value)
            place(e, z, kme)[...] = value

        for j in range(1, 4):
            rcopy(place(e, z, kme), place(e, z, kme), yg_sems.at[e, kme], ydev[j], cond=own)

    def sib_send(e, o, k, n, i):
        rcopy(place(e, o, k, n), place(e, o, k, n), sb_sems.at[e, i], sibling)

    def ag_first(e):
        for k in range(3):

            @pl.when(yowner(k) != y)
            def _():
                arrived(place(e, z, k), yg_sems.at[e, k])

        piece = place(e, z, 0, 3)
        for d in range(2):
            rcopy(piece, piece, ag_sems.at[e, d, 1], zdev2[d])
        for d in range(2):
            rcopy(piece, piece, ag_sems.at[e, d, 0], zdev[d])
        sib_send(e, z, 0, 3, 0)

    def ag_second(e):
        for d in range(2):
            k, n = far[d]
            o = (z - 2 * sgn[d] + 8) % 8
            piece = place(e, o, 0, 3)
            arrived(piece, ag_sems.at[e, d, 1])
            rcopy(piece, piece, ag_sems.at[e, d, 2], zdev[d])
            rcopy(place(e, o, k, n), place(e, o, k, n), ag_sems.at[e, d, 3], zdev2[d])
            sib_send(e, o, 0, 3, 1 + d)
        for d in range(2):
            o = (z - sgn[d] + 8) % 8
            arrived(place(e, o, 0, 3), ag_sems.at[e, d, 0])
            sib_send(e, o, 0, 3, 3 + d)

    def ag_last(e):
        for d in range(2):
            o = (z - 3 * sgn[d] + 8) % 8
            arrived(place(e, o, 0, 3), ag_sems.at[e, d, 2])
            sib_send(e, o, 0, 3, 5 + d)
        o = (z + 4) % 8
        for d in range(2):
            k, n = far[d]
            arrived(place(e, o, k, n), ag_sems.at[e, d, 3])
            sib_send(e, o, k, n, 7 + d)

    def sib_wait(e):
        def place_sib(o, k, n):
            row = TOK + TOK * (o // 4) + 96 * (o % 2) + 48 * (1 - c) + 16 * k
            return KV.at[e, (o // 2) % 2, pl.ds(pl.multiple_of(row, 16), 16 * n)]

        arrived(place_sib(z, 0, 3), sb_sems.at[e, 0])
        for d in range(2):
            for base, dist in ((1, 2), (3, 1), (5, 3)):
                o = (z - dist * sgn[1 - d] + 8) % 8
                arrived(place_sib(o, 0, 3), sb_sems.at[e, base + d])
            k, n = far[d]
            arrived(place_sib((z + 4) % 8, k, n), sb_sems.at[e, 7 + d])

    lam = step_ref[0].astype(F32) / STEPS

    def heads(e):
        def one(g, carry):
            cols = pl.ds(pl.multiple_of(g * HD, HD), HD)
            q = Q[e, :, cols]
            keys = KV[e, 0, :, cols]
            vals = KV[e, 1, :, cols]
            s = lax.dot_general(q, keys, (((1,), (1,)), ((), ())), preferred_element_type=F32)
            p = jnp.exp2(s - jnp.max(s, axis=1, keepdims=True)).astype(BF)
            both = jnp.concatenate([vals, jnp.ones((3 * TOK, HD), BF)], axis=1)
            o = lax.dot_general(p, both, (((1,), (0,)), ((), ())), preferred_element_type=F32)
            o = (o[:, :HD] / o[:, HD:]).astype(BF)
            if e == 0:
                OH[:, cols] = o
            else:
                mixed = (1.0 - lam) * OH[:, cols].astype(F32) + lam * o.astype(F32)
                pad = jnp.zeros((8, HD), F32)
                for p8 in range(8):
                    rows = mixed[LOCAL * p8 : LOCAL * p8 + LOCAL]
                    MB[p8, :, cols] = jnp.concatenate([rows, pad], axis=0).astype(BF)
            return carry

        lax.fori_loop(0, 5, one, 0)

    def low_keys():
        for j in range(1, 8):
            arrived(RKV.at[hidx[j]], akv_sems.at[hidx[j]])
        for p in range(4):
            a = RKV[2 * p].astype(F32)
            b = RKV[2 * p + 1].astype(F32)
            rows = slice(48 * p, 48 * p + 48)
            KV[1, 0, rows] = jnp.concatenate([a[:LOCAL], b[:LOCAL]], axis=0).astype(BF)
            KV[1, 1, rows] = jnp.concatenate([a[LOCAL:], b[LOCAL:]], axis=0).astype(BF)

    def low_queries():
        for j in range(1, 8):
            arrived(RQ.at[hidx[j]], aq_sems.at[hidx[j]])
        for p in range(4):
            a = RQ[2 * p].astype(F32)
            b = RQ[2 * p + 1].astype(F32)
            Q[1, 48 * p : 48 * p + 48] = jnp.concatenate([a[:LOCAL], b[:LOCAL]], axis=0).astype(BF)

    gather_pair(0)
    rs_first(0)
    low_keys()
    h1_send(1, 0)
    h1_send(1, 1)
    rs_second(0)
    gather_pair(1)
    rs_first(1)
    y_send(0)
    rs_second(1)
    y_own(0)
    ag_first(0)
    low_queries()
    y_send(1)
    ag_second(0)
    y_own(1)
    ag_last(0)
    ag_first(1)
    sib_wait(0)
    ag_second(1)
    heads(0)
    ag_last(1)
    sib_wait(1)
    heads(1)

    RB[h] = MB[h]
    for j in range(1, 8):
        rcopy(MB.at[hidx[j]], RB.at[h], back_sems.at[h], hdev[j])
    for j in range(1, 8):
        arrived(RB.at[hidx[j]], back_sems.at[hidx[j]])
    for p in range(8):
        out[:, W * p : W * p + W] = RB[p, 0:LOCAL]

    for copy, cond in ends:
        if cond is None:
            copy.wait_send()
        else:
            pl.when(cond)(copy.wait_send)


def body(
    q_high,
    k_high,
    v_high,
    gain_qh,
    gain_kh,
    q_low,
    k_low,
    v_low,
    gain_ql,
    gain_kl,
    keyframes,
    switch_step,
    permutation,
):
    smem = pl.BlockSpec(memory_space=pltpu.SMEM)
    vmem = pl.BlockSpec(memory_space=pltpu.VMEM)
    hbm = pl.BlockSpec(memory_space=pl.ANY)
    dma = pltpu.SemaphoreType.DMA
    return pl.pallas_call(
        kernel,
        out_shape=jax.ShapeDtypeStruct((LOCAL, WIDTH), BF),
        in_specs=[smem, smem] + [hbm] * 11,
        out_specs=vmem,
        scratch_shapes=[
            pltpu.VMEM((TOK, W), BF),
            pltpu.VMEM((TOK, W), BF),
            pltpu.VMEM((LOCAL, WIDTH), BF),
            pltpu.VMEM((LOCAL, WIDTH), BF),
            pltpu.VMEM((LOCAL, WIDTH), BF),
            pltpu.VMEM((W,), F32),
            pltpu.VMEM((W,), F32),
            pltpu.VMEM((WIDTH,), F32),
            pltpu.VMEM((WIDTH,), F32),
            pltpu.VMEM((TOK,), jnp.int32),
            pltpu.VMEM((2, 2, 3 * TOK, W), BF),
            pltpu.VMEM((2, TOK, W), BF),
            pltpu.VMEM((TOK, W), BF),
            pltpu.VMEM((2, 8, 48, W), BF),
            pltpu.VMEM((2, 2, 2, 48, W), BF),
            pltpu.VMEM((2, 2, 4, 48, W), BF),
            pltpu.VMEM((2, 3, 16, W), BF),
            pltpu.VMEM((2, 4, 16, W), BF),
            pltpu.VMEM((8, 48, W), BF),
            pltpu.VMEM((8, 48, W), BF),
            pltpu.VMEM((8, 32, W), BF),
            pltpu.VMEM((8, 32, W), BF),
            pltpu.VMEM((8, TOK), F32),
            pltpu.VMEM((8, 8, TOK), F32),
            pltpu.VMEM((8, 32, W), BF),
            pltpu.VMEM((8, 32, W), BF),
            dma((11,)),
            dma((120,)),
            dma((8,)),
            dma((8,)),
            dma((8,)),
            dma((8,)),
            dma((2, 2, 2)),
            dma((2, 2, 4)),
            dma((2, 4)),
            dma((2, 4)),
            dma((2, 2, 4)),
            dma((2, 9)),
        ],
        compiler_params=pltpu.CompilerParams(
            collective_id=0, has_side_effects=True, vmem_limit_bytes=56 * 1024 * 1024
        ),
    )(
        keyframes,
        switch_step,
        q_high,
        k_high,
        v_high,
        gain_qh,
        gain_kh,
        q_low,
        k_low,
        v_low,
        gain_ql,
        gain_kl,
        permutation,
    )


def solution(mesh):
    return jax.shard_map(
        body,
        mesh=mesh,
        in_specs=(
            P("frame", "head"),
            P("frame", "head"),
            P("frame", "head"),
            P("head"),
            P("head"),
            P(("frame", "head"), None),
            P(("frame", "head"), None),
            P(("frame", "head"), None),
            P(),
            P(),
            P(),
            P(),
            P(),
        ),
        out_specs=P(("frame", "head"), None),
        check_vma=False,
    )
```

```python
import functools
import math

import jax
import jax.numpy as jnp
from jax import lax
from jax.experimental import pallas as pl
from jax.experimental.pallas import tpu as pltpu
from jax.sharding import PartitionSpec as P

HEADS = 40
HD = 128
STEPS = 40
EPS = 1e-06
TOK = 192
W = 640
WIDTH = HEADS * HD
LOCAL = 24
BF = jnp.bfloat16
F32 = jnp.float32
MESH = pl.DeviceIdType.MESH
GROUPS = ((0, 2), (2, 4), (4, 5))
QSCALE = HD ** (-0.5) * math.log2(math.e)


def kernel(
    kf_hbm,
    step_hbm,
    q_high_hbm,
    k_high_hbm,
    v_high_hbm,
    gain_qh_hbm,
    gain_kh_hbm,
    q_low_hbm,
    k_low_hbm,
    v_low_hbm,
    gain_ql_hbm,
    gain_kl_hbm,
    perm_hbm,
    out,
    kf,
    step_ref,
    q_high,
    q_low,
    k_low,
    v_low,
    gain_qh,
    gain_kh,
    gain_ql,
    gain_kl,
    perm,
    KV,
    Q,
    OH,
    CH,
    H1R,
    RZ,
    ZC,
    RY,
    SKV,
    RKV,
    SQ,
    RQ,
    SS,
    RS,
    FO,
    FS,
    FC,
    FZ,
    FY,
    FK,
    MB,
    RB,
    load_sems,
    send_sems,
    sum_sems,
    fs_sems,
    fz_sems,
    fy_sems,
    akv_sems,
    aq_sems,
    back_sems,
    h1_sems,
    rz_sems,
    ry_sems,
    yg_sems,
    ag_sems,
    sb_sems,
):
    f = lax.axis_index("frame")
    h = lax.axis_index("head")
    z = f // 8
    y = (f // 2) % 4
    c = f % 2
    sgn = (1 - 2 * c, 2 * c - 1)

    def at(zz, yy, cc, hh):
        return {"frame": (zz * 4 + yy) * 2 + cc, "head": hh}

    def zat(distance):
        return (z + distance + 8) % 8

    sibling = at(z, y, 1 - c, h)
    zdev = [at(zat(s), y, c, h) for s in sgn]
    zdev2 = [at(zat(2 * s), y, c, h) for s in sgn]
    zidx = [zat(j) for j in range(8)]
    zall = [at(zidx[j], y, c, h) for j in range(8)]
    yidx = [(y + j) % 4 for j in range(4)]
    ydev = [at(z, yidx[j], c, h) for j in range(4)]
    hidx = [(h + j) % 8 for j in range(8)]
    hdev = [at(z, y, c, hidx[j]) for j in range(8)]

    barrier = pltpu.get_barrier_semaphore()
    partners = [sibling] + zall[1:] + ydev[1:] + hdev[1:]
    for dev in partners:
        pl.semaphore_signal(barrier, inc=1, device_id=dev, device_id_type=MESH)

    loads = {}
    for name, src, dst in (
        ("kh", k_high_hbm, KV.at[0, 0, pl.ds(0, TOK)]),
        ("vh", v_high_hbm, KV.at[0, 1, pl.ds(0, TOK)]),
        ("kf", kf_hbm, kf),
        ("kl", k_low_hbm, k_low),
        ("vl", v_low_hbm, v_low),
        ("gkl", gain_kl_hbm, gain_kl),
        ("qh", q_high_hbm, q_high),
        ("ql", q_low_hbm, q_low),
        ("gql", gain_ql_hbm, gain_ql),
        ("gkh", gain_kh_hbm, gain_kh),
        ("gqh", gain_qh_hbm, gain_qh),
        ("perm", perm_hbm, perm),
        ("step", step_hbm, step_ref),
    ):
        loads[name] = pltpu.make_async_copy(src, dst, load_sems.at[len(loads)])
        loads[name].start()

    def loaded(*names):
        for name in names:
            loads[name].wait()

    count = [0]
    ends = []

    def rcopy(src, dst, rsem, dev, cond=None):
        index = count[0]
        count[0] += 1
        copy = pltpu.make_async_remote_copy(
            src_ref=src,
            dst_ref=dst,
            send_sem=send_sems.at[index],
            recv_sem=rsem,
            device_id=dev,
            device_id_type=MESH,
        )
        if cond is None:
            copy.start()
        else:
            pl.when(cond)(copy.start)
        ends.append((copy, cond))

    def arrived(dst, rsem, cond=None):
        copy = pltpu.make_async_remote_copy(
            src_ref=dst,
            dst_ref=dst,
            send_sem=send_sems.at[0],
            recv_sem=rsem,
            device_id=sibling,
            device_id_type=MESH,
        )
        if cond is None:
            copy.wait_recv()
        else:
            pl.when(cond)(copy.wait_recv)

    def chunk(k, n=1):
        return pl.ds(16 * k, 16 * n)

    def held(e, o, k, n, core):
        row = TOK + TOK * (o // 4) + 96 * (o % 2) + 48 * core + 16 * k
        return KV.at[e, (o // 2) % 2, pl.ds(pl.multiple_of(row, 16), 16 * n)]

    def place(e, o, k, n=1):
        return held(e, o, k, n, c)

    def root_of(o):
        return jnp.where(o // 4 == 0, kf[0], kf[1])

    def h1_rows(rh, core):
        return pl.ds(pl.multiple_of(96 * rh + 48 * core, 16), 48)

    def h1_send(e):
        for kv in range(2):
            for rh in range(2):
                rcopy(
                    KV.at[e, kv, h1_rows(rh, 1 - c)],
                    H1R.at[e, kv, rh],
                    h1_sems.at[e, kv, rh],
                    sibling,
                )

    def gather_pair(e):
        for kv in range(2):
            for rh in range(2):
                arrived(H1R.at[e, kv, rh], h1_sems.at[e, kv, rh])
                mine = KV[e, kv, h1_rows(rh, c)]
                other = H1R[e, kv, rh]
                for s in range(2):
                    CH[e, s * 4 + kv * 2 + rh] = jnp.where(kf[s] % 2 == c, mine, other)

    far = ((0, 1), (2,))

    def rs_first(e):
        for k in range(3):
            for d in range(2):
                o3, o4 = zat(3 * sgn[d]), zat(4)
                if k in far[d]:
                    rcopy(CH.at[e, o4, chunk(k)], RZ.at[e, d, 1, chunk(k)], rz_sems.at[e, d, 1, k], zdev2[d])
                rcopy(CH.at[e, o3, chunk(k)], RZ.at[e, d, 0, chunk(k)], rz_sems.at[e, d, 0, k], zdev[d])
        for k in range(3):
            for d in range(2):
                o1 = zat(sgn[d])
                rcopy(CH.at[e, o1, chunk(k)], RZ.at[e, d, 2, chunk(k)], rz_sems.at[e, d, 2, k], zdev[d])

    def rs_second(e):
        for k in range(3):
            for d in range(2):
                o2 = zat(2 * sgn[d])
                away = ((z - root_of(o2) // 8) * sgn[d] + 8) % 8
                arrived(RZ.at[e, d, 0, chunk(k)], rz_sems.at[e, d, 0, k])
                value = jnp.where(away == 0, CH[e, o2, chunk(k)], RZ[e, d, 0, chunk(k)])
                if k in far[d]:
                    arrived(RZ.at[e, d, 1, chunk(k)], rz_sems.at[e, d, 1, k])
                    value = jnp.where(away == 2, RZ[e, d, 1, chunk(k)], value)
                RZ[e, d, 0, chunk(k)] = value
                rcopy(RZ.at[e, d, 0, chunk(k)], RZ.at[e, d, 3, chunk(k)], rz_sems.at[e, d, 3, k], zdev2[d])

    def yowner(k):
        return (k + 2 * c) % 4

    def y_send(e):
        away = ((z - root_of(z) // 8) * sgn[0] + 8) % 8
        for k in range(3):
            for d in range(2):
                arrived(RZ.at[e, d, 2, chunk(k)], rz_sems.at[e, d, 2, k])
                arrived(RZ.at[e, d, 3, chunk(k)], rz_sems.at[e, d, 3, k])
            limit = 5 if k in far[0] else 4
            value = jnp.where(away == 1, RZ[e, 0, 2, chunk(k)], RZ[e, 0, 3, chunk(k)])
            value = jnp.where(away >= limit, RZ[e, 1, 3, chunk(k)], value)
            value = jnp.where(away == 7, RZ[e, 1, 2, chunk(k)], value)
            ZC[e, k] = jnp.where(away == 0, CH[e, z, chunk(k)], value)
            yo = yowner(k)
            rcopy(ZC.at[e, k], RY.at[e, y], ry_sems.at[e, y], at(z, yo, c, h), cond=yo != y)

    kown = (y - 2 * c + 4) % 4
    own = kown < 3
    kme = jnp.minimum(kown, 2)
    order = [(kme + j) % 3 for j in range(3)]

    def y_own(e):
        @pl.when(own)
        def _():
            for j in range(1, 4):
                arrived(RY.at[e, yidx[j]], ry_sems.at[e, yidx[j]])
            RY[e, y] = ZC[e, kme]
            root = (root_of(z) // 2) % 4
            value = RY[e, 0]
            for yy in range(1, 4):
                value = jnp.where(root == yy, RY[e, yy], value)
            place(e, z, kme)[...] = value

        piece = place(e, z, kme)
        for j in range(1, 4):
            rcopy(piece, piece, yg_sems.at[e, kme], ydev[j], cond=own)

    def sib_send(e, o, k, i):
        piece = place(e, o, k)
        rcopy(piece, piece, sb_sems.at[e, i, k], sibling)

    def ag_first(e):
        for k in order:
            piece = place(e, z, k)
            arrived(piece, yg_sems.at[e, k], cond=yowner(k) != y)
            for d in range(2):
                rcopy(piece, piece, ag_sems.at[e, d, 1, k], zdev2[d])
            for d in range(2):
                rcopy(piece, piece, ag_sems.at[e, d, 0, k], zdev[d])
            sib_send(e, z, k, 0)

    def ag_second(e):
        for k in order:
            for d in range(2):
                piece = place(e, zat(-2 * sgn[d]), k)
                arrived(piece, ag_sems.at[e, d, 1, k])
                rcopy(piece, piece, ag_sems.at[e, d, 3, k], zdev2[d], cond=k < 2 if d == 0 else k == 2)
                rcopy(piece, piece, ag_sems.at[e, d, 2, k], zdev[d])
                sib_send(e, zat(-2 * sgn[d]), k, 1 + d)
        for k in order:
            for d in range(2):
                arrived(place(e, zat(-sgn[d]), k), ag_sems.at[e, d, 0, k])
                sib_send(e, zat(-sgn[d]), k, 3 + d)

    def ag_last(e):
        for k in order:
            for d in range(2):
                arrived(place(e, zat(-3 * sgn[d]), k), ag_sems.at[e, d, 2, k])
                sib_send(e, zat(-3 * sgn[d]), k, 5 + d)
            piece = place(e, zat(4), k)
            for d in range(2):
                arrived(piece, ag_sems.at[e, d, 3, k], cond=k < 2 if d == 0 else k == 2)
            sib_send(e, zat(4), k, 7)

    def sib_wait(e):
        for k in range(3):
            arrived(held(e, z, k, 1, 1 - c), sb_sems.at[e, 0, k])
            for d in range(2):
                for base, dist in ((1, 2), (3, 1), (5, 3)):
                    arrived(held(e, zat(-dist * sgn[1 - d]), k, 1, 1 - c), sb_sems.at[e, base + d, k])
            arrived(held(e, zat(4), k, 1, 1 - c), sb_sems.at[e, 7, k])

    def rows_sum(values):
        x = values.astype(F32)
        x = x * x
        hi = x.astype(BF)
        lo = (x - hi.astype(F32)).astype(BF)
        ones = jnp.ones((8, W), BF)
        dims = (((1,), (1,)), ((), ()))
        return lax.dot_general(ones, hi, dims, preferred_element_type=F32) + lax.dot_general(
            ones, lo, dims, preferred_element_type=F32
        )

    def factor(ref):
        x = ref[...].astype(F32)
        return lax.rsqrt(jnp.sum(x * x, axis=1, keepdims=True) / WIDTH + EPS)

    def low_keys_pack():
        loaded("kl", "vl", "gkl")
        fk = factor(k_low)
        for p in range(8):
            cols = slice(W * p, W * p + W)
            kn = k_low[:, cols].astype(F32) * fk * gain_kl[cols].reshape(1, W)
            SKV[p] = jnp.concatenate([kn, v_low[:, cols].astype(F32)], axis=0).astype(BF)
        RKV[h] = SKV[h]

    def low_queries_pack():
        loaded("ql", "gql")
        fq = factor(q_low)
        for p in range(8):
            cols = slice(W * p, W * p + W)
            qn = q_low[:, cols].astype(F32) * (fq * QSCALE) * gain_ql[cols].reshape(1, W)
            SQ[p] = jnp.concatenate([qn, jnp.zeros((8, W), F32)], axis=0).astype(BF)
        RQ[h] = SQ[h]

    def low_keys():
        for j in range(1, 8):
            arrived(RKV.at[hidx[j]], akv_sems.at[hidx[j]])
        for p in range(4):
            a = RKV[2 * p].astype(F32)
            b = RKV[2 * p + 1].astype(F32)
            rows = slice(48 * p, 48 * p + 48)
            KV[1, 0, rows] = jnp.concatenate([a[:LOCAL], b[:LOCAL]], axis=0).astype(BF)
            KV[1, 1, rows] = jnp.concatenate([a[LOCAL:], b[LOCAL:]], axis=0).astype(BF)

    def low_queries():
        for j in range(1, 8):
            arrived(RQ.at[hidx[j]], aq_sems.at[hidx[j]])
        for p in range(4):
            a = RQ[2 * p].astype(F32)
            b = RQ[2 * p + 1].astype(F32)
            Q[1, 48 * p : 48 * p + 48] = jnp.concatenate([a[:LOCAL], b[:LOCAL]], axis=0).astype(BF)

    def factors():
        for j in range(1, 8):
            arrived(RS.at[hidx[j]], sum_sems.at[hidx[j]])
        total = RS[0]
        for p in range(1, 8):
            total = total + RS[p]
        FO[...] = lax.rsqrt(total / WIDTH + EPS)
        rcopy(FO, FS, fs_sems.at[0], sibling)

    def factors_z():
        arrived(FS, fs_sems.at[0])
        key = lax.broadcasted_iota(jnp.int32, (8, TOK), 0) - 4
        pick = [jnp.where(kf[s] % 2 == c, FO[...], FS[...]) for s in range(2)]
        FC[...] = jnp.where(key == 0, pick[0], pick[1])
        for j in (4, 3, 5, 2, 6, 1, 7):
            rcopy(FC, FZ.at[z], fz_sems.at[z], zall[j])

    def by_slot(values, roots):
        row = lax.broadcasted_iota(jnp.int32, (8, TOK), 0)
        key = jnp.where(row == 4, roots[0], roots[1])
        total = values[0]
        for i in range(1, len(values)):
            total = jnp.where(key == i, values[i], total)
        return total

    def factors_y():
        FZ[z] = FC[...]
        for j in range(1, 8):
            arrived(FZ.at[zidx[j]], fz_sems.at[zidx[j]])
        FY[y] = by_slot([FZ[i] for i in range(8)], [kf[s] // 8 for s in range(2)])
        for j in range(1, 4):
            rcopy(FY.at[y], FY.at[y], fy_sems.at[y], ydev[j])

    def factors_done():
        for j in range(1, 4):
            arrived(FY.at[yidx[j]], fy_sems.at[yidx[j]])
        FK[...] = by_slot([FY[i] for i in range(4)], [(kf[s] // 2) % 4 for s in range(2)])

    def high_queries():
        loaded("gkh", "gqh", "perm")
        pick = jnp.where(lax.broadcasted_iota(jnp.int32, (8, HD), 0) == 0, QSCALE, 0.0)
        qfac = lax.dot_general(
            FO[...],
            pick,
            (((0,), (0,)), ((), ())),
            precision=lax.Precision.HIGHEST,
            preferred_element_type=F32,
        )
        token = lax.broadcasted_iota(jnp.int32, (TOK, TOK), 0)
        hot = jnp.where(token == perm[...].reshape(1, TOK), 1.0, 0.0).astype(BF)
        for g in range(5):
            cols = slice(HD * g, HD * g + HD)
            gains = (gain_qh[cols] * gain_kh[cols]).reshape(1, HD)
            qn = (q_high[:, cols].astype(F32) * qfac * gains).astype(BF)
            Q[0, :, cols] = lax.dot_general(
                hot, qn, (((0,), (0,)), ((), ())), preferred_element_type=F32
            ).astype(BF)

    def attend(e, cols):
        s = lax.dot_general(
            Q[e, :, cols],
            KV[e, 0, :, cols],
            (((1,), (1,)), ((), ())),
            preferred_element_type=F32,
        )
        if e == 0:
            s = s * jnp.concatenate([FO[4:5], FK[4:5], FK[5:6]], axis=1)
        p = jnp.exp2(s - jnp.max(s, axis=1, keepdims=True)).astype(BF)
        both = jnp.concatenate([KV[e, 1, :, cols], jnp.ones((3 * TOK, HD), BF)], axis=1)
        o = lax.dot_general(p, both, (((1,), (0,)), ((), ())), preferred_element_type=F32)
        return (o[:, :HD] / o[:, HD:]).astype(BF)

    def high_heads():
        def one(g, carry):
            cols = pl.ds(pl.multiple_of(g * HD, HD), HD)
            OH[:, cols] = attend(0, cols)
            return carry

        lax.fori_loop(0, 5, one, 0)

    def low_heads():
        loaded("step")
        lam = step_ref[0].astype(F32) / STEPS
        for i, (start, stop) in enumerate(GROUPS):

            def one(g, carry):
                cols = pl.ds(pl.multiple_of(g * HD, HD), HD)
                mixed = (1.0 - lam) * OH[:, cols].astype(F32) + lam * attend(1, cols).astype(F32)
                pad = jnp.zeros((8, HD), F32)
                for p in range(8):
                    rows = mixed[LOCAL * p : LOCAL * p + LOCAL]
                    MB[p, :, cols] = jnp.concatenate([rows, pad], axis=0).astype(BF)
                return carry

            lax.fori_loop(start, stop, one, 0)
            cols = pl.ds(HD * start, HD * (stop - start))
            for j in range(1, 8):
                rcopy(MB.at[hidx[j], :, cols], RB.at[h, :, cols], back_sems.at[i, h], hdev[j])

    low_keys_pack()
    loaded("kh", "vh", "kf")
    pl.semaphore_wait(barrier, len(partners))
    h1_send(0)
    for j in range(1, 8):
        rcopy(SKV.at[hidx[j]], RKV.at[h], akv_sems.at[h], hdev[j])
    loaded("qh")
    half = lax.broadcasted_iota(jnp.int32, (8, TOK), 0)
    SS[...] = jnp.where(half < 4, rows_sum(q_high[...]), rows_sum(KV[0, 0, 0:TOK]))
    RS[h] = SS[...]
    for j in range(1, 8):
        rcopy(SS, RS.at[h], sum_sems.at[h], hdev[j])
    gather_pair(0)
    rs_first(0)
    low_queries_pack()
    for j in range(1, 8):
        rcopy(SQ.at[hidx[j]], RQ.at[h], aq_sems.at[h], hdev[j])
    factors()
    rs_second(0)
    low_keys()
    h1_send(1)
    factors_z()
    high_queries()
    y_send(0)
    gather_pair(1)
    rs_first(1)
    y_own(0)
    factors_y()
    rs_second(1)
    ag_first(0)
    low_queries()
    y_send(1)
    ag_second(0)
    y_own(1)
    factors_done()
    ag_last(0)
    ag_first(1)
    sib_wait(0)
    ag_second(1)
    high_heads()
    ag_last(1)
    sib_wait(1)
    low_heads()

    RB[h] = MB[h]
    for j in range(1, 8):
        for i, (start, stop) in enumerate(GROUPS):
            cols = pl.ds(HD * start, HD * (stop - start))
            arrived(RB.at[hidx[j], :, cols], back_sems.at[i, hidx[j]])
    for p in range(8):
        out[:, W * p : W * p + W] = RB[p, 0:LOCAL]

    for copy, cond in ends:
        if cond is None:
            copy.wait_send()
        else:
            pl.when(cond)(copy.wait_send)


def body(
    q_high,
    k_high,
    v_high,
    gain_qh,
    gain_kh,
    q_low,
    k_low,
    v_low,
    gain_ql,
    gain_kl,
    keyframes,
    switch_step,
    permutation,
):
    vmem = pl.BlockSpec(memory_space=pltpu.VMEM)
    hbm = pl.BlockSpec(memory_space=pl.ANY)
    dma = pltpu.SemaphoreType.DMA
    return pl.pallas_call(
        kernel,
        out_shape=jax.ShapeDtypeStruct((LOCAL, WIDTH), BF),
        in_specs=[hbm] * 13,
        out_specs=vmem,
        scratch_shapes=[
            pltpu.SMEM((2,), jnp.int32),
            pltpu.SMEM((1,), jnp.int32),
            pltpu.VMEM((TOK, W), BF),
            pltpu.VMEM((LOCAL, WIDTH), BF),
            pltpu.VMEM((LOCAL, WIDTH), BF),
            pltpu.VMEM((LOCAL, WIDTH), BF),
            pltpu.VMEM((W,), F32),
            pltpu.VMEM((W,), F32),
            pltpu.VMEM((WIDTH,), F32),
            pltpu.VMEM((WIDTH,), F32),
            pltpu.VMEM((TOK,), jnp.int32),
            pltpu.VMEM((2, 2, 3 * TOK, W), BF),
            pltpu.VMEM((2, TOK, W), BF),
            pltpu.VMEM((TOK, W), BF),
            pltpu.VMEM((2, 8, 48, W), BF),
            pltpu.VMEM((2, 2, 2, 48, W), BF),
            pltpu.VMEM((2, 2, 4, 48, W), BF),
            pltpu.VMEM((2, 3, 16, W), BF),
            pltpu.VMEM((2, 4, 16, W), BF),
            pltpu.VMEM((8, 48, W), BF),
            pltpu.VMEM((8, 48, W), BF),
            pltpu.VMEM((8, 32, W), BF),
            pltpu.VMEM((8, 32, W), BF),
            pltpu.VMEM((8, TOK), F32),
            pltpu.VMEM((8, 8, TOK), F32),
            pltpu.VMEM((8, TOK), F32),
            pltpu.VMEM((8, TOK), F32),
            pltpu.VMEM((8, TOK), F32),
            pltpu.VMEM((8, 8, TOK), F32),
            pltpu.VMEM((4, 8, TOK), F32),
            pltpu.VMEM((8, TOK), F32),
            pltpu.VMEM((8, 32, W), BF),
            pltpu.VMEM((8, 32, W), BF),
            dma((13,)),
            dma((280,)),
            dma((8,)),
            dma((1,)),
            dma((8,)),
            dma((4,)),
            dma((8,)),
            dma((8,)),
            dma((3, 8)),
            dma((2, 2, 2)),
            dma((2, 2, 4, 3)),
            dma((2, 4)),
            dma((2, 3)),
            dma((2, 2, 4, 3)),
            dma((2, 8, 3)),
        ],
        compiler_params=pltpu.CompilerParams(
            collective_id=0, has_side_effects=True, vmem_limit_bytes=56 * 1024 * 1024
        ),
    )(
        keyframes,
        switch_step,
        q_high,
        k_high,
        v_high,
        gain_qh,
        gain_kh,
        q_low,
        k_low,
        v_low,
        gain_ql,
        gain_kl,
        permutation,
    )


def solution(mesh):
    return jax.shard_map(
        body,
        mesh=mesh,
        in_specs=(
            P("frame", "head"),
            P("frame", "head"),
            P("frame", "head"),
            P("head"),
            P("head"),
            P(("frame", "head"), None),
            P(("frame", "head"), None),
            P(("frame", "head"), None),
            P(),
            P(),
            P(),
            P(),
            P(),
        ),
        out_specs=P(("frame", "head"), None),
        check_vma=False,
    )
```

```python
import functools
import math

import jax
import jax.numpy as jnp
from jax import lax
from jax.experimental import pallas as pl
from jax.experimental.pallas import tpu as pltpu
from jax.sharding import PartitionSpec as P

HEADS = 40
HD = 128
STEPS = 40
EPS = 1e-06
TOK = 192
W = 640
WIDTH = HEADS * HD
LOCAL = 24
BF = jnp.bfloat16
F32 = jnp.float32
MESH = pl.DeviceIdType.MESH
GROUPS = ((0, 2), (2, 4), (4, 5))
QSCALE = HD ** (-0.5) * math.log2(math.e)


def kernel(
    kf_hbm,
    step_hbm,
    q_high_hbm,
    k_high_hbm,
    v_high_hbm,
    gain_qh_hbm,
    gain_kh_hbm,
    q_low_hbm,
    k_low_hbm,
    v_low_hbm,
    gain_ql_hbm,
    gain_kl_hbm,
    perm_hbm,
    out,
    kf,
    step_ref,
    q_high,
    q_low,
    k_low,
    v_low,
    gain_qh,
    gain_kh,
    gain_ql,
    gain_kl,
    perm,
    KV,
    Q,
    OH,
    CH,
    H1R,
    RZ,
    ZC,
    RY,
    SKV,
    RKV,
    SQ,
    RQ,
    SS,
    RS,
    FO,
    FS,
    FC,
    FZ,
    FY,
    FK,
    MB,
    RB,
    load_sems,
    send_sems,
    sum_sems,
    fs_sems,
    fz_sems,
    fy_sems,
    akv_sems,
    aq_sems,
    back_sems,
    h1_sems,
    rz_sems,
    ry_sems,
    yg_sems,
    ag_sems,
    sb_sems,
):
    f = lax.axis_index("frame")
    h = lax.axis_index("head")
    z = f // 8
    y = (f // 2) % 4
    c = f % 2
    sgn = (1 - 2 * c, 2 * c - 1)

    def at(zz, yy, cc, hh):
        return {"frame": (zz * 4 + yy) * 2 + cc, "head": hh}

    def zat(distance):
        return (z + distance + 8) % 8

    sibling = at(z, y, 1 - c, h)
    zdev = [at(zat(s), y, c, h) for s in sgn]
    zdev2 = [at(zat(2 * s), y, c, h) for s in sgn]
    zidx = [zat(j) for j in range(8)]
    zall = [at(zidx[j], y, c, h) for j in range(8)]
    yidx = [(y + j) % 4 for j in range(4)]
    ydev = [at(z, yidx[j], c, h) for j in range(4)]
    hidx = [(h + j) % 8 for j in range(8)]
    hdev = [at(z, y, c, hidx[j]) for j in range(8)]

    barrier = pltpu.get_barrier_semaphore()
    partners = [sibling] + zall[1:] + ydev[1:] + hdev[1:]
    for dev in partners:
        pl.semaphore_signal(barrier, inc=1, device_id=dev, device_id_type=MESH)

    loads = {}
    for name, src, dst in (
        ("kh", k_high_hbm, KV.at[0, 0, pl.ds(0, TOK)]),
        ("vh", v_high_hbm, KV.at[0, 1, pl.ds(0, TOK)]),
        ("kf", kf_hbm, kf),
        ("kl", k_low_hbm, k_low),
        ("vl", v_low_hbm, v_low),
        ("gkl", gain_kl_hbm, gain_kl),
        ("qh", q_high_hbm, q_high),
        ("ql", q_low_hbm, q_low),
        ("gql", gain_ql_hbm, gain_ql),
        ("gkh", gain_kh_hbm, gain_kh),
        ("gqh", gain_qh_hbm, gain_qh),
        ("perm", perm_hbm, perm),
        ("step", step_hbm, step_ref),
    ):
        loads[name] = pltpu.make_async_copy(src, dst, load_sems.at[len(loads)])
        loads[name].start()

    def loaded(*names):
        for name in names:
            loads[name].wait()

    count = [0]
    ends = []

    def rcopy(src, dst, rsem, dev, cond=None):
        index = count[0]
        count[0] += 1
        copy = pltpu.make_async_remote_copy(
            src_ref=src,
            dst_ref=dst,
            send_sem=send_sems.at[index],
            recv_sem=rsem,
            device_id=dev,
            device_id_type=MESH,
        )
        if cond is None:
            copy.start()
        else:
            pl.when(cond)(copy.start)
        ends.append((copy, cond))

    def arrived(dst, rsem, cond=None):
        copy = pltpu.make_async_remote_copy(
            src_ref=dst,
            dst_ref=dst,
            send_sem=send_sems.at[0],
            recv_sem=rsem,
            device_id=sibling,
            device_id_type=MESH,
        )
        if cond is None:
            copy.wait_recv()
        else:
            pl.when(cond)(copy.wait_recv)

    def chunk(k, n=1):
        return pl.ds(16 * k, 16 * n)

    def held(e, o, k, n, core):
        row = TOK + TOK * (o // 4) + 96 * (o % 2) + 48 * core + 16 * k
        return KV.at[e, (o // 2) % 2, pl.ds(pl.multiple_of(row, 16), 16 * n)]

    def place(e, o, k, n=1):
        return held(e, o, k, n, c)

    def root_of(o):
        return jnp.where(o // 4 == 0, kf[0], kf[1])

    def h1_rows(rh, core):
        return pl.ds(pl.multiple_of(96 * rh + 48 * core, 16), 48)

    def h1_send(e):
        for kv in range(2):
            for rh in range(2):
                rcopy(
                    KV.at[e, kv, h1_rows(rh, 1 - c)],
                    H1R.at[e, kv, rh],
                    h1_sems.at[e, kv, rh],
                    sibling,
                )

    def gather_pair(e):
        for kv in range(2):
            for rh in range(2):
                arrived(H1R.at[e, kv, rh], h1_sems.at[e, kv, rh])
                mine = KV[e, kv, h1_rows(rh, c)]
                other = H1R[e, kv, rh]
                for s in range(2):
                    CH[e, s * 4 + kv * 2 + rh] = jnp.where(kf[s] % 2 == c, mine, other)

    far = ((0, 1), (2,))

    def rs_first(e):
        for k in range(3):
            for d in range(2):
                o3, o4 = zat(3 * sgn[d]), zat(4)
                if k in far[d]:
                    rcopy(CH.at[e, o4, chunk(k)], RZ.at[e, d, 1, chunk(k)], rz_sems.at[e, d, 1, k], zdev2[d])
                rcopy(CH.at[e, o3, chunk(k)], RZ.at[e, d, 0, chunk(k)], rz_sems.at[e, d, 0, k], zdev[d])
        for k in range(3):
            for d in range(2):
                o1 = zat(sgn[d])
                rcopy(CH.at[e, o1, chunk(k)], RZ.at[e, d, 2, chunk(k)], rz_sems.at[e, d, 2, k], zdev[d])

    def rs_second(e):
        for k in range(3):
            for d in range(2):
                o2 = zat(2 * sgn[d])
                away = ((z - root_of(o2) // 8) * sgn[d] + 8) % 8
                arrived(RZ.at[e, d, 0, chunk(k)], rz_sems.at[e, d, 0, k])
                value = jnp.where(away == 0, CH[e, o2, chunk(k)], RZ[e, d, 0, chunk(k)])
                if k in far[d]:
                    arrived(RZ.at[e, d, 1, chunk(k)], rz_sems.at[e, d, 1, k])
                    value = jnp.where(away == 2, RZ[e, d, 1, chunk(k)], value)
                RZ[e, d, 0, chunk(k)] = value
                rcopy(RZ.at[e, d, 0, chunk(k)], RZ.at[e, d, 3, chunk(k)], rz_sems.at[e, d, 3, k], zdev2[d])

    def yowner(k):
        return (k + 2 * c) % 4

    def y_send(e):
        away = ((z - root_of(z) // 8) * sgn[0] + 8) % 8
        for k in range(3):
            for d in range(2):
                arrived(RZ.at[e, d, 2, chunk(k)], rz_sems.at[e, d, 2, k])
                arrived(RZ.at[e, d, 3, chunk(k)], rz_sems.at[e, d, 3, k])
            limit = 5 if k in far[0] else 4
            value = jnp.where(away == 1, RZ[e, 0, 2, chunk(k)], RZ[e, 0, 3, chunk(k)])
            value = jnp.where(away >= limit, RZ[e, 1, 3, chunk(k)], value)
            value = jnp.where(away == 7, RZ[e, 1, 2, chunk(k)], value)
            ZC[e, k] = jnp.where(away == 0, CH[e, z, chunk(k)], value)
            yo = yowner(k)
            rcopy(ZC.at[e, k], RY.at[e, y], ry_sems.at[e, y], at(z, yo, c, h), cond=yo != y)

    kown = (y - 2 * c + 4) % 4
    own = kown < 3
    kme = jnp.minimum(kown, 2)
    order = [(kme + j) % 3 for j in range(3)]

    def y_own(e):
        @pl.when(own)
        def _():
            for j in range(1, 4):
                arrived(RY.at[e, yidx[j]], ry_sems.at[e, yidx[j]])
            RY[e, y] = ZC[e, kme]
            root = (root_of(z) // 2) % 4
            value = RY[e, 0]
            for yy in range(1, 4):
                value = jnp.where(root == yy, RY[e, yy], value)
            place(e, z, kme)[...] = value

        piece = place(e, z, kme)
        for j in range(1, 4):
            rcopy(piece, piece, yg_sems.at[e, kme], ydev[j], cond=own)

    def sib_send(e, o, k, i):
        piece = place(e, o, k)
        rcopy(piece, piece, sb_sems.at[e, i, k], sibling)

    def ag_first(e):
        for k in order:
            piece = place(e, z, k)
            arrived(piece, yg_sems.at[e, k], cond=yowner(k) != y)
            for d in range(2):
                rcopy(piece, piece, ag_sems.at[e, d, 1, k], zdev2[d])
            for d in range(2):
                rcopy(piece, piece, ag_sems.at[e, d, 0, k], zdev[d])
            sib_send(e, z, k, 0)

    def ag_second(e):
        for k in order:
            for d in range(2):
                piece = place(e, zat(-2 * sgn[d]), k)
                arrived(piece, ag_sems.at[e, d, 1, k])
                rcopy(piece, piece, ag_sems.at[e, d, 3, k], zdev2[d], cond=k < 2 if d == 0 else k == 2)
                rcopy(piece, piece, ag_sems.at[e, d, 2, k], zdev[d])
                sib_send(e, zat(-2 * sgn[d]), k, 1 + d)
        for k in order:
            for d in range(2):
                arrived(place(e, zat(-sgn[d]), k), ag_sems.at[e, d, 0, k])
                sib_send(e, zat(-sgn[d]), k, 3 + d)

    def ag_last(e):
        for k in order:
            for d in range(2):
                arrived(place(e, zat(-3 * sgn[d]), k), ag_sems.at[e, d, 2, k])
                sib_send(e, zat(-3 * sgn[d]), k, 5 + d)
            piece = place(e, zat(4), k)
            for d in range(2):
                arrived(piece, ag_sems.at[e, d, 3, k], cond=k < 2 if d == 0 else k == 2)
            sib_send(e, zat(4), k, 7)

    def sib_wait(e):
        for k in range(3):
            arrived(held(e, z, k, 1, 1 - c), sb_sems.at[e, 0, k])
            for d in range(2):
                for base, dist in ((1, 2), (3, 1), (5, 3)):
                    arrived(held(e, zat(-dist * sgn[1 - d]), k, 1, 1 - c), sb_sems.at[e, base + d, k])
            arrived(held(e, zat(4), k, 1, 1 - c), sb_sems.at[e, 7, k])

    def rows_sum(values):
        x = values.astype(F32)
        x = x * x
        hi = x.astype(BF)
        lo = (x - hi.astype(F32)).astype(BF)
        ones = jnp.ones((8, W), BF)
        dims = (((1,), (1,)), ((), ()))
        return lax.dot_general(ones, hi, dims, preferred_element_type=F32) + lax.dot_general(
            ones, lo, dims, preferred_element_type=F32
        )

    def factor(ref):
        x = ref[...].astype(F32)
        return lax.rsqrt(jnp.sum(x * x, axis=1, keepdims=True) / WIDTH + EPS)

    def low_keys_pack():
        loaded("kl", "vl", "gkl")
        fk = factor(k_low)
        for p in range(8):
            cols = slice(W * p, W * p + W)
            kn = k_low[:, cols].astype(F32) * fk * gain_kl[cols].reshape(1, W)
            SKV[p] = jnp.concatenate([kn, v_low[:, cols].astype(F32)], axis=0).astype(BF)
        RKV[h] = SKV[h]

    def low_queries_pack():
        loaded("ql", "gql")
        fq = factor(q_low)
        for p in range(8):
            cols = slice(W * p, W * p + W)
            qn = q_low[:, cols].astype(F32) * (fq * QSCALE) * gain_ql[cols].reshape(1, W)
            SQ[p] = jnp.concatenate([qn, jnp.zeros((8, W), F32)], axis=0).astype(BF)
        RQ[h] = SQ[h]

    def low_keys():
        for j in range(1, 8):
            arrived(RKV.at[hidx[j]], akv_sems.at[hidx[j]])
        for p in range(4):
            a = RKV[2 * p].astype(F32)
            b = RKV[2 * p + 1].astype(F32)
            rows = slice(48 * p, 48 * p + 48)
            KV[1, 0, rows] = jnp.concatenate([a[:LOCAL], b[:LOCAL]], axis=0).astype(BF)
            KV[1, 1, rows] = jnp.concatenate([a[LOCAL:], b[LOCAL:]], axis=0).astype(BF)

    def low_queries():
        for j in range(1, 8):
            arrived(RQ.at[hidx[j]], aq_sems.at[hidx[j]])
        for p in range(4):
            a = RQ[2 * p].astype(F32)
            b = RQ[2 * p + 1].astype(F32)
            Q[1, 48 * p : 48 * p + 48] = jnp.concatenate([a[:LOCAL], b[:LOCAL]], axis=0).astype(BF)

    def factors():
        for j in range(1, 8):
            arrived(RS.at[hidx[j]], sum_sems.at[hidx[j]])
        total = RS[0]
        for p in range(1, 8):
            total = total + RS[p]
        FO[...] = lax.rsqrt(total / WIDTH + EPS)
        rcopy(FO, FS, fs_sems.at[0], sibling)

    def factors_z():
        arrived(FS, fs_sems.at[0])
        key = lax.broadcasted_iota(jnp.int32, (8, TOK), 0) - 4
        pick = [jnp.where(kf[s] % 2 == c, FO[...], FS[...]) for s in range(2)]
        FC[...] = jnp.where(key == 0, pick[0], pick[1])
        for j in (4, 3, 5, 2, 6, 1, 7):
            rcopy(FC, FZ.at[z], fz_sems.at[z], zall[j])

    def by_slot(values, roots):
        row = lax.broadcasted_iota(jnp.int32, (8, TOK), 0)
        key = jnp.where(row == 4, roots[0], roots[1])
        total = values[0]
        for i in range(1, len(values)):
            total = jnp.where(key == i, values[i], total)
        return total

    def factors_y():
        FZ[z] = FC[...]
        for j in range(1, 8):
            arrived(FZ.at[zidx[j]], fz_sems.at[zidx[j]])
        FY[y] = by_slot([FZ[i] for i in range(8)], [kf[s] // 8 for s in range(2)])
        for j in range(1, 4):
            rcopy(FY.at[y], FY.at[y], fy_sems.at[y], ydev[j])

    def factors_done():
        for j in range(1, 4):
            arrived(FY.at[yidx[j]], fy_sems.at[yidx[j]])
        FK[...] = by_slot([FY[i] for i in range(4)], [(kf[s] // 2) % 4 for s in range(2)])

    def high_queries():
        loaded("gkh", "gqh", "perm")
        pick = jnp.where(lax.broadcasted_iota(jnp.int32, (8, HD), 0) == 0, QSCALE, 0.0)
        qfac = lax.dot_general(
            FO[...],
            pick,
            (((0,), (0,)), ((), ())),
            precision=lax.Precision.HIGHEST,
            preferred_element_type=F32,
        )
        token = lax.broadcasted_iota(jnp.int32, (TOK, TOK), 0)
        hot = jnp.where(token == perm[...].reshape(1, TOK), 1.0, 0.0).astype(BF)
        for g in range(5):
            cols = slice(HD * g, HD * g + HD)
            gains = (gain_qh[cols] * gain_kh[cols]).reshape(1, HD)
            qn = (q_high[:, cols].astype(F32) * qfac * gains).astype(BF)
            Q[0, :, cols] = lax.dot_general(
                hot, qn, (((0,), (0,)), ((), ())), preferred_element_type=F32
            ).astype(BF)

    def attend(e, cols):
        s = lax.dot_general(
            Q[e, :, cols],
            KV[e, 0, :, cols],
            (((1,), (1,)), ((), ())),
            preferred_element_type=F32,
        )
        if e == 0:
            s = s * jnp.concatenate([FO[4:5], FK[4:5], FK[5:6]], axis=1)
        p = jnp.exp2(s - jnp.max(s, axis=1, keepdims=True)).astype(BF)
        both = jnp.concatenate([KV[e, 1, :, cols], jnp.ones((3 * TOK, HD), BF)], axis=1)
        o = lax.dot_general(p, both, (((1,), (0,)), ((), ())), preferred_element_type=F32)
        return (o[:, :HD] / o[:, HD:]).astype(BF)

    def high_heads():
        def one(g, carry):
            cols = pl.ds(pl.multiple_of(g * HD, HD), HD)
            OH[:, cols] = attend(0, cols)
            return carry

        lax.fori_loop(0, 5, one, 0, unroll=True)

    def low_heads():
        loaded("step")
        lam = step_ref[0].astype(F32) / STEPS
        for i, (start, stop) in enumerate(GROUPS):

            def one(g, carry):
                cols = pl.ds(pl.multiple_of(g * HD, HD), HD)
                mixed = (1.0 - lam) * OH[:, cols].astype(F32) + lam * attend(1, cols).astype(F32)
                pad = jnp.zeros((8, HD), F32)
                for p in range(8):
                    rows = mixed[LOCAL * p : LOCAL * p + LOCAL]
                    MB[p, :, cols] = jnp.concatenate([rows, pad], axis=0).astype(BF)
                return carry

            lax.fori_loop(start, stop, one, 0, unroll=True)
            cols = pl.ds(HD * start, HD * (stop - start))
            for j in range(1, 8):
                rcopy(MB.at[hidx[j], :, cols], RB.at[h, :, cols], back_sems.at[i, h], hdev[j])

    low_keys_pack()
    loaded("kh", "vh", "kf")
    pl.semaphore_wait(barrier, len(partners))
    h1_send(0)
    for j in range(1, 8):
        rcopy(SKV.at[hidx[j]], RKV.at[h], akv_sems.at[h], hdev[j])
    loaded("qh")
    half = lax.broadcasted_iota(jnp.int32, (8, TOK), 0)
    SS[...] = jnp.where(half < 4, rows_sum(q_high[...]), rows_sum(KV[0, 0, 0:TOK]))
    RS[h] = SS[...]
    for j in range(1, 8):
        rcopy(SS, RS.at[h], sum_sems.at[h], hdev[j])
    gather_pair(0)
    rs_first(0)
    low_queries_pack()
    factors()
    rs_second(0)
    low_keys()
    h1_send(1)
    factors_z()
    gather_pair(1)
    rs_first(1)
    y_send(0)
    high_queries()
    rs_second(1)
    factors_y()
    y_own(0)
    y_send(1)
    ag_first(0)
    y_own(1)
    for j in range(1, 8):
        rcopy(SQ.at[hidx[j]], RQ.at[h], aq_sems.at[h], hdev[j])
    ag_second(0)
    factors_done()
    ag_first(1)
    ag_last(0)
    ag_second(1)
    sib_wait(0)
    low_queries()
    high_heads()
    ag_last(1)
    sib_wait(1)
    low_heads()

    def sent(copies):
        for copy, cond in copies:
            if cond is None:
                copy.wait_send()
            else:
                pl.when(cond)(copy.wait_send)

    late = 7 * len(GROUPS)
    sent(ends[:-late])
    RB[h] = MB[h]
    for j in range(1, 8):
        for i, (start, stop) in enumerate(GROUPS):
            cols = pl.ds(HD * start, HD * (stop - start))
            arrived(RB.at[hidx[j], :, cols], back_sems.at[i, hidx[j]])
    for p in range(8):
        out[:, W * p : W * p + W] = RB[p, 0:LOCAL]

    sent(ends[-late:])


def body(
    q_high,
    k_high,
    v_high,
    gain_qh,
    gain_kh,
    q_low,
    k_low,
    v_low,
    gain_ql,
    gain_kl,
    keyframes,
    switch_step,
    permutation,
):
    vmem = pl.BlockSpec(memory_space=pltpu.VMEM)
    hbm = pl.BlockSpec(memory_space=pl.ANY)
    dma = pltpu.SemaphoreType.DMA
    return pl.pallas_call(
        kernel,
        out_shape=jax.ShapeDtypeStruct((LOCAL, WIDTH), BF),
        in_specs=[hbm] * 13,
        out_specs=vmem,
        scratch_shapes=[
            pltpu.SMEM((2,), jnp.int32),
            pltpu.SMEM((1,), jnp.int32),
            pltpu.VMEM((TOK, W), BF),
            pltpu.VMEM((LOCAL, WIDTH), BF),
            pltpu.VMEM((LOCAL, WIDTH), BF),
            pltpu.VMEM((LOCAL, WIDTH), BF),
            pltpu.VMEM((W,), F32),
            pltpu.VMEM((W,), F32),
            pltpu.VMEM((WIDTH,), F32),
            pltpu.VMEM((WIDTH,), F32),
            pltpu.VMEM((TOK,), jnp.int32),
            pltpu.VMEM((2, 2, 3 * TOK, W), BF),
            pltpu.VMEM((2, TOK, W), BF),
            pltpu.VMEM((TOK, W), BF),
            pltpu.VMEM((2, 8, 48, W), BF),
            pltpu.VMEM((2, 2, 2, 48, W), BF),
            pltpu.VMEM((2, 2, 4, 48, W), BF),
            pltpu.VMEM((2, 3, 16, W), BF),
            pltpu.VMEM((2, 4, 16, W), BF),
            pltpu.VMEM((8, 48, W), BF),
            pltpu.VMEM((8, 48, W), BF),
            pltpu.VMEM((8, 32, W), BF),
            pltpu.VMEM((8, 32, W), BF),
            pltpu.VMEM((8, TOK), F32),
            pltpu.VMEM((8, 8, TOK), F32),
            pltpu.VMEM((8, TOK), F32),
            pltpu.VMEM((8, TOK), F32),
            pltpu.VMEM((8, TOK), F32),
            pltpu.VMEM((8, 8, TOK), F32),
            pltpu.VMEM((4, 8, TOK), F32),
            pltpu.VMEM((8, TOK), F32),
            pltpu.VMEM((8, 32, W), BF),
            pltpu.VMEM((8, 32, W), BF),
            dma((13,)),
            dma((280,)),
            dma((8,)),
            dma((1,)),
            dma((8,)),
            dma((4,)),
            dma((8,)),
            dma((8,)),
            dma((3, 8)),
            dma((2, 2, 2)),
            dma((2, 2, 4, 3)),
            dma((2, 4)),
            dma((2, 3)),
            dma((2, 2, 4, 3)),
            dma((2, 8, 3)),
        ],
        compiler_params=pltpu.CompilerParams(
            collective_id=0, has_side_effects=True, vmem_limit_bytes=56 * 1024 * 1024
        ),
    )(
        keyframes,
        switch_step,
        q_high,
        k_high,
        v_high,
        gain_qh,
        gain_kh,
        q_low,
        k_low,
        v_low,
        gain_ql,
        gain_kl,
        permutation,
    )


def solution(mesh):
    return jax.shard_map(
        body,
        mesh=mesh,
        in_specs=(
            P("frame", "head"),
            P("frame", "head"),
            P("frame", "head"),
            P("head"),
            P("head"),
            P(("frame", "head"), None),
            P(("frame", "head"), None),
            P(("frame", "head"), None),
            P(),
            P(),
            P(),
            P(),
            P(),
        ),
        out_specs=P(("frame", "head"), None),
        check_vma=False,
    )
```

```python
import functools
import math

import jax
import jax.numpy as jnp
from jax import lax
from jax.experimental import pallas as pl
from jax.experimental.pallas import tpu as pltpu
from jax.sharding import PartitionSpec as P

HEADS = 40
HD = 128
STEPS = 40
EPS = 1e-06
TOK = 192
W = 640
WIDTH = HEADS * HD
LOCAL = 24
BF = jnp.bfloat16
F32 = jnp.float32
MESH = pl.DeviceIdType.MESH
GROUPS = ((0, 2), (2, 4), (4, 5))
QSCALE = HD ** (-0.5) * math.log2(math.e)


def kernel(
    kf_hbm,
    step_hbm,
    q_high_hbm,
    k_high_hbm,
    v_high_hbm,
    gain_qh_hbm,
    gain_kh_hbm,
    q_low_hbm,
    k_low_hbm,
    v_low_hbm,
    gain_ql_hbm,
    gain_kl_hbm,
    perm_hbm,
    out,
    kf,
    step_ref,
    q_high,
    q_low,
    k_low,
    v_low,
    gain_qh,
    gain_kh,
    gain_ql,
    gain_kl,
    perm,
    KV,
    Q,
    OH,
    CH,
    H1R,
    RZ,
    ZC,
    RY,
    SKV,
    RKV,
    SQ,
    RQ,
    SS,
    RS,
    FO,
    FS,
    FC,
    FZ,
    FY,
    FK,
    MB,
    RB,
    load_sems,
    send_sems,
    sum_sems,
    fs_sems,
    fz_sems,
    fy_sems,
    akv_sems,
    aq_sems,
    back_sems,
    h1_sems,
    rz_sems,
    ry_sems,
    yg_sems,
    ag_sems,
    sb_sems,
):
    f = lax.axis_index("frame")
    h = lax.axis_index("head")
    z = f // 8
    y = (f // 2) % 4
    c = f % 2
    sgn = (1 - 2 * c, 2 * c - 1)

    def at(zz, yy, cc, hh):
        return {"frame": (zz * 4 + yy) * 2 + cc, "head": hh}

    def zat(distance):
        return (z + distance + 8) % 8

    sibling = at(z, y, 1 - c, h)
    zdev = [at(zat(s), y, c, h) for s in sgn]
    zdev2 = [at(zat(2 * s), y, c, h) for s in sgn]
    zidx = [zat(j) for j in range(8)]
    zall = [at(zidx[j], y, c, h) for j in range(8)]
    yidx = [(y + j) % 4 for j in range(4)]
    ydev = [at(z, yidx[j], c, h) for j in range(4)]
    hops = ((0, 0), (2, 1), (2, 0), (1, 1), (3, 1), (1, 0), (3, 0), (0, 1))
    hidx = [((h // 2 + dx) % 4) * 2 + (h + dl) % 2 for dx, dl in hops]
    hdev = [at(z, y, c, hidx[j]) for j in range(8)]

    barrier = pltpu.get_barrier_semaphore()
    partners = [sibling] + zall[1:] + ydev[1:] + hdev[1:]
    for dev in partners:
        pl.semaphore_signal(barrier, inc=1, device_id=dev, device_id_type=MESH)

    loads = {}
    for name, src, dst in (
        ("kh", k_high_hbm, KV.at[0, 0, pl.ds(0, TOK)]),
        ("vh", v_high_hbm, KV.at[0, 1, pl.ds(0, TOK)]),
        ("kf", kf_hbm, kf),
        ("kl", k_low_hbm, k_low),
        ("vl", v_low_hbm, v_low),
        ("gkl", gain_kl_hbm, gain_kl),
        ("qh", q_high_hbm, q_high),
        ("ql", q_low_hbm, q_low),
        ("gql", gain_ql_hbm, gain_ql),
        ("gkh", gain_kh_hbm, gain_kh),
        ("gqh", gain_qh_hbm, gain_qh),
        ("perm", perm_hbm, perm),
        ("step", step_hbm, step_ref),
    ):
        loads[name] = pltpu.make_async_copy(src, dst, load_sems.at[len(loads)])
        loads[name].start()

    def loaded(*names):
        for name in names:
            loads[name].wait()

    count = [0]
    ends = []

    def rcopy(src, dst, rsem, dev, cond=None):
        index = count[0]
        count[0] += 1
        copy = pltpu.make_async_remote_copy(
            src_ref=src,
            dst_ref=dst,
            send_sem=send_sems.at[index],
            recv_sem=rsem,
            device_id=dev,
            device_id_type=MESH,
        )
        if cond is None:
            copy.start()
        else:
            pl.when(cond)(copy.start)
        ends.append((copy, cond))

    def arrived(dst, rsem, cond=None):
        copy = pltpu.make_async_remote_copy(
            src_ref=dst,
            dst_ref=dst,
            send_sem=send_sems.at[0],
            recv_sem=rsem,
            device_id=sibling,
            device_id_type=MESH,
        )
        if cond is None:
            copy.wait_recv()
        else:
            pl.when(cond)(copy.wait_recv)

    def chunk(k, n=1):
        return pl.ds(16 * k, 16 * n)

    def held(e, o, k, n, core):
        row = TOK + TOK * (o // 4) + 96 * (o % 2) + 48 * core + 16 * k
        return KV.at[e, (o // 2) % 2, pl.ds(pl.multiple_of(row, 16), 16 * n)]

    def place(e, o, k, n=1):
        return held(e, o, k, n, c)

    def root_of(o):
        return jnp.where(o // 4 == 0, kf[0], kf[1])

    def h1_rows(rh, core):
        return pl.ds(pl.multiple_of(96 * rh + 48 * core, 16), 48)

    def h1_send(e):
        for kv in range(2):
            for rh in range(2):
                rcopy(
                    KV.at[e, kv, h1_rows(rh, 1 - c)],
                    H1R.at[e, kv, rh],
                    h1_sems.at[e, kv, rh],
                    sibling,
                )

    def gather_pair(e):
        for kv in range(2):
            for rh in range(2):
                arrived(H1R.at[e, kv, rh], h1_sems.at[e, kv, rh])
                mine = KV[e, kv, h1_rows(rh, c)]
                other = H1R[e, kv, rh]
                for s in range(2):
                    CH[e, s * 4 + kv * 2 + rh] = jnp.where(kf[s] % 2 == c, mine, other)

    far = ((0, 1), (2,))

    def rs_first(e):
        for k in range(3):
            for d in range(2):
                o3, o4 = zat(3 * sgn[d]), zat(4)
                if k in far[d]:
                    rcopy(CH.at[e, o4, chunk(k)], RZ.at[e, d, 1, chunk(k)], rz_sems.at[e, d, 1, k], zdev2[d])
                rcopy(CH.at[e, o3, chunk(k)], RZ.at[e, d, 0, chunk(k)], rz_sems.at[e, d, 0, k], zdev[d])
        for k in range(3):
            for d in range(2):
                o1 = zat(sgn[d])
                rcopy(CH.at[e, o1, chunk(k)], RZ.at[e, d, 2, chunk(k)], rz_sems.at[e, d, 2, k], zdev[d])

    def rs_second(e):
        for k in range(3):
            for d in range(2):
                o2 = zat(2 * sgn[d])
                away = ((z - root_of(o2) // 8) * sgn[d] + 8) % 8
                arrived(RZ.at[e, d, 0, chunk(k)], rz_sems.at[e, d, 0, k])
                value = jnp.where(away == 0, CH[e, o2, chunk(k)], RZ[e, d, 0, chunk(k)])
                if k in far[d]:
                    arrived(RZ.at[e, d, 1, chunk(k)], rz_sems.at[e, d, 1, k])
                    value = jnp.where(away == 2, RZ[e, d, 1, chunk(k)], value)
                RZ[e, d, 0, chunk(k)] = value
                rcopy(RZ.at[e, d, 0, chunk(k)], RZ.at[e, d, 3, chunk(k)], rz_sems.at[e, d, 3, k], zdev2[d])

    def yowner(k):
        return (k + 2 * c) % 4

    def y_send(e):
        away = ((z - root_of(z) // 8) * sgn[0] + 8) % 8
        for k in range(3):
            for d in range(2):
                arrived(RZ.at[e, d, 2, chunk(k)], rz_sems.at[e, d, 2, k])
                arrived(RZ.at[e, d, 3, chunk(k)], rz_sems.at[e, d, 3, k])
            limit = 5 if k in far[0] else 4
            value = jnp.where(away == 1, RZ[e, 0, 2, chunk(k)], RZ[e, 0, 3, chunk(k)])
            value = jnp.where(away >= limit, RZ[e, 1, 3, chunk(k)], value)
            value = jnp.where(away == 7, RZ[e, 1, 2, chunk(k)], value)
            ZC[e, k] = jnp.where(away == 0, CH[e, z, chunk(k)], value)
            yo = yowner(k)
            rcopy(ZC.at[e, k], RY.at[e, y], ry_sems.at[e, y], at(z, yo, c, h), cond=yo != y)

    kown = (y - 2 * c + 4) % 4
    own = kown < 3
    kme = jnp.minimum(kown, 2)
    order = [(kme + j) % 3 for j in range(3)]

    def y_own(e):
        @pl.when(own)
        def _():
            for j in range(1, 4):
                arrived(RY.at[e, yidx[j]], ry_sems.at[e, yidx[j]])
            RY[e, y] = ZC[e, kme]
            root = (root_of(z) // 2) % 4
            value = RY[e, 0]
            for yy in range(1, 4):
                value = jnp.where(root == yy, RY[e, yy], value)
            place(e, z, kme)[...] = value

        piece = place(e, z, kme)
        for j in range(1, 4):
            rcopy(piece, piece, yg_sems.at[e, kme], ydev[j], cond=own)

    def sib_send(e, o, k, i):
        piece = place(e, o, k)
        rcopy(piece, piece, sb_sems.at[e, i, k], sibling)

    def ag_first(e):
        for k in order:
            piece = place(e, z, k)
            arrived(piece, yg_sems.at[e, k], cond=yowner(k) != y)
            for d in range(2):
                rcopy(piece, piece, ag_sems.at[e, d, 1, k], zdev2[d])
            for d in range(2):
                rcopy(piece, piece, ag_sems.at[e, d, 0, k], zdev[d])
            sib_send(e, z, k, 0)

    def ag_second(e):
        for k in order:
            for d in range(2):
                piece = place(e, zat(-2 * sgn[d]), k)
                arrived(piece, ag_sems.at[e, d, 1, k])
                rcopy(piece, piece, ag_sems.at[e, d, 3, k], zdev2[d], cond=k < 2 if d == 0 else k == 2)
                rcopy(piece, piece, ag_sems.at[e, d, 2, k], zdev[d])
                sib_send(e, zat(-2 * sgn[d]), k, 1 + d)
        for k in order:
            for d in range(2):
                arrived(place(e, zat(-sgn[d]), k), ag_sems.at[e, d, 0, k])
                sib_send(e, zat(-sgn[d]), k, 3 + d)

    def ag_last(e):
        for k in order:
            for d in range(2):
                arrived(place(e, zat(-3 * sgn[d]), k), ag_sems.at[e, d, 2, k])
                sib_send(e, zat(-3 * sgn[d]), k, 5 + d)
            piece = place(e, zat(4), k)
            for d in range(2):
                arrived(piece, ag_sems.at[e, d, 3, k], cond=k < 2 if d == 0 else k == 2)
            sib_send(e, zat(4), k, 7)

    def sib_wait(e):
        for k in range(3):
            arrived(held(e, z, k, 1, 1 - c), sb_sems.at[e, 0, k])
            for d in range(2):
                for base, dist in ((1, 2), (3, 1), (5, 3)):
                    arrived(held(e, zat(-dist * sgn[1 - d]), k, 1, 1 - c), sb_sems.at[e, base + d, k])
            arrived(held(e, zat(4), k, 1, 1 - c), sb_sems.at[e, 7, k])

    def rows_sum(values):
        x = values.astype(F32)
        x = x * x
        hi = x.astype(BF)
        lo = (x - hi.astype(F32)).astype(BF)
        ones = jnp.ones((8, W), BF)
        dims = (((1,), (1,)), ((), ()))
        return lax.dot_general(ones, hi, dims, preferred_element_type=F32) + lax.dot_general(
            ones, lo, dims, preferred_element_type=F32
        )

    def factor(ref):
        x = ref[...].astype(F32)
        return lax.rsqrt(jnp.sum(x * x, axis=1, keepdims=True) / WIDTH + EPS)

    def low_keys_pack():
        loaded("kl", "vl", "gkl")
        fk = factor(k_low)
        for p in range(8):
            cols = slice(W * p, W * p + W)
            kn = k_low[:, cols].astype(F32) * fk * gain_kl[cols].reshape(1, W)
            SKV[p] = jnp.concatenate([kn, v_low[:, cols].astype(F32)], axis=0).astype(BF)
        RKV[h] = SKV[h]

    def low_queries_pack():
        loaded("ql", "gql")
        fq = factor(q_low)
        for p in range(8):
            cols = slice(W * p, W * p + W)
            qn = q_low[:, cols].astype(F32) * (fq * QSCALE) * gain_ql[cols].reshape(1, W)
            SQ[p] = jnp.concatenate([qn, jnp.zeros((8, W), F32)], axis=0).astype(BF)
        RQ[h] = SQ[h]

    def low_keys():
        for j in range(1, 8):
            arrived(RKV.at[hidx[j]], akv_sems.at[hidx[j]])
        for p in range(4):
            a = RKV[2 * p].astype(F32)
            b = RKV[2 * p + 1].astype(F32)
            rows = slice(48 * p, 48 * p + 48)
            KV[1, 0, rows] = jnp.concatenate([a[:LOCAL], b[:LOCAL]], axis=0).astype(BF)
            KV[1, 1, rows] = jnp.concatenate([a[LOCAL:], b[LOCAL:]], axis=0).astype(BF)

    def low_queries():
        for j in range(1, 8):
            arrived(RQ.at[hidx[j]], aq_sems.at[hidx[j]])
        for p in range(4):
            a = RQ[2 * p].astype(F32)
            b = RQ[2 * p + 1].astype(F32)
            Q[1, 48 * p : 48 * p + 48] = jnp.concatenate([a[:LOCAL], b[:LOCAL]], axis=0).astype(BF)

    def factors():
        for j in range(1, 8):
            arrived(RS.at[hidx[j]], sum_sems.at[hidx[j]])
        total = RS[0]
        for p in range(1, 8):
            total = total + RS[p]
        FO[...] = lax.rsqrt(total / WIDTH + EPS)
        rcopy(FO, FS, fs_sems.at[0], sibling)

    def factors_z():
        arrived(FS, fs_sems.at[0])
        key = lax.broadcasted_iota(jnp.int32, (8, TOK), 0) - 4
        pick = [jnp.where(kf[s] % 2 == c, FO[...], FS[...]) for s in range(2)]
        FC[...] = jnp.where(key == 0, pick[0], pick[1])
        for j in (4, 3, 5, 2, 6, 1, 7):
            rcopy(FC, FZ.at[z], fz_sems.at[z], zall[j])

    def by_slot(values, roots):
        row = lax.broadcasted_iota(jnp.int32, (8, TOK), 0)
        key = jnp.where(row == 4, roots[0], roots[1])
        total = values[0]
        for i in range(1, len(values)):
            total = jnp.where(key == i, values[i], total)
        return total

    def factors_y():
        FZ[z] = FC[...]
        for j in range(1, 8):
            arrived(FZ.at[zidx[j]], fz_sems.at[zidx[j]])
        FY[y] = by_slot([FZ[i] for i in range(8)], [kf[s] // 8 for s in range(2)])
        for j in range(1, 4):
            rcopy(FY.at[y], FY.at[y], fy_sems.at[y], ydev[j])

    def factors_done():
        for j in range(1, 4):
            arrived(FY.at[yidx[j]], fy_sems.at[yidx[j]])
        FK[...] = by_slot([FY[i] for i in range(4)], [(kf[s] // 2) % 4 for s in range(2)])

    def high_queries():
        loaded("gkh", "gqh", "perm")
        pick = jnp.where(lax.broadcasted_iota(jnp.int32, (8, HD), 0) == 0, QSCALE, 0.0)
        qfac = lax.dot_general(
            FO[...],
            pick,
            (((0,), (0,)), ((), ())),
            precision=lax.Precision.HIGHEST,
            preferred_element_type=F32,
        )
        token = lax.broadcasted_iota(jnp.int32, (TOK, TOK), 0)
        hot = jnp.where(token == perm[...].reshape(1, TOK), 1.0, 0.0).astype(BF)
        for g in range(5):
            cols = slice(HD * g, HD * g + HD)
            gains = (gain_qh[cols] * gain_kh[cols]).reshape(1, HD)
            qn = (q_high[:, cols].astype(F32) * qfac * gains).astype(BF)
            Q[0, :, cols] = lax.dot_general(
                hot, qn, (((0,), (0,)), ((), ())), preferred_element_type=F32
            ).astype(BF)

    def attend(e, cols):
        s = lax.dot_general(
            Q[e, :, cols],
            KV[e, 0, :, cols],
            (((1,), (1,)), ((), ())),
            preferred_element_type=F32,
        )
        if e == 0:
            s = s * jnp.concatenate([FO[4:5], FK[4:5], FK[5:6]], axis=1)
        p = jnp.exp2(s - jnp.max(s, axis=1, keepdims=True)).astype(BF)
        both = jnp.concatenate([KV[e, 1, :, cols], jnp.ones((3 * TOK, HD), BF)], axis=1)
        o = lax.dot_general(p, both, (((1,), (0,)), ((), ())), preferred_element_type=F32)
        return (o[:, :HD] / o[:, HD:]).astype(BF)

    def high_heads():
        def one(g, carry):
            cols = pl.ds(pl.multiple_of(g * HD, HD), HD)
            OH[:, cols] = attend(0, cols)
            return carry

        lax.fori_loop(0, 5, one, 0, unroll=True)

    def low_heads():
        loaded("step")
        lam = step_ref[0].astype(F32) / STEPS
        for i, (start, stop) in enumerate(GROUPS):

            def one(g, carry):
                cols = pl.ds(pl.multiple_of(g * HD, HD), HD)
                mixed = (1.0 - lam) * OH[:, cols].astype(F32) + lam * attend(1, cols).astype(F32)
                pad = jnp.zeros((8, HD), F32)
                for p in range(8):
                    rows = mixed[LOCAL * p : LOCAL * p + LOCAL]
                    MB[p, :, cols] = jnp.concatenate([rows, pad], axis=0).astype(BF)
                return carry

            lax.fori_loop(start, stop, one, 0, unroll=True)
            cols = pl.ds(HD * start, HD * (stop - start))
            for j in range(1, 8):
                rcopy(MB.at[hidx[j], :, cols], RB.at[h, :, cols], back_sems.at[i, h], hdev[j])

    low_keys_pack()
    loaded("kh", "vh", "kf")
    pl.semaphore_wait(barrier, len(partners))
    for j in range(1, 8):
        rcopy(SKV.at[hidx[j]], RKV.at[h], akv_sems.at[h], hdev[j])
    h1_send(0)
    loaded("qh")
    half = lax.broadcasted_iota(jnp.int32, (8, TOK), 0)
    SS[...] = jnp.where(half < 4, rows_sum(q_high[...]), rows_sum(KV[0, 0, 0:TOK]))
    RS[h] = SS[...]
    for j in range(1, 8):
        rcopy(SS, RS.at[h], sum_sems.at[h], hdev[j])
    gather_pair(0)
    rs_first(0)
    low_queries_pack()
    rs_second(0)
    low_keys()
    h1_send(1)
    gather_pair(1)
    rs_first(1)
    y_send(0)
    rs_second(1)
    factors()
    y_own(0)
    y_send(1)
    factors_z()
    ag_first(0)
    high_queries()
    y_own(1)
    for j in range(1, 8):
        rcopy(SQ.at[hidx[j]], RQ.at[h], aq_sems.at[h], hdev[j])
    factors_y()
    ag_first(1)
    ag_second(0)
    ag_second(1)
    factors_done()
    ag_last(0)
    sib_wait(0)
    low_queries()
    high_heads()
    ag_last(1)
    sib_wait(1)
    low_heads()

    def sent(copies):
        for copy, cond in copies:
            if cond is None:
                copy.wait_send()
            else:
                pl.when(cond)(copy.wait_send)

    late = 7 * len(GROUPS)
    sent(ends[:-late])
    RB[h] = MB[h]
    for j in range(1, 8):
        for i, (start, stop) in enumerate(GROUPS):
            cols = pl.ds(HD * start, HD * (stop - start))
            arrived(RB.at[hidx[j], :, cols], back_sems.at[i, hidx[j]])
    for p in range(8):
        out[:, W * p : W * p + W] = RB[p, 0:LOCAL]

    sent(ends[-late:])


def body(
    q_high,
    k_high,
    v_high,
    gain_qh,
    gain_kh,
    q_low,
    k_low,
    v_low,
    gain_ql,
    gain_kl,
    keyframes,
    switch_step,
    permutation,
):
    vmem = pl.BlockSpec(memory_space=pltpu.VMEM)
    hbm = pl.BlockSpec(memory_space=pl.ANY)
    dma = pltpu.SemaphoreType.DMA
    return pl.pallas_call(
        kernel,
        out_shape=jax.ShapeDtypeStruct((LOCAL, WIDTH), BF),
        in_specs=[hbm] * 13,
        out_specs=vmem,
        scratch_shapes=[
            pltpu.SMEM((2,), jnp.int32),
            pltpu.SMEM((1,), jnp.int32),
            pltpu.VMEM((TOK, W), BF),
            pltpu.VMEM((LOCAL, WIDTH), BF),
            pltpu.VMEM((LOCAL, WIDTH), BF),
            pltpu.VMEM((LOCAL, WIDTH), BF),
            pltpu.VMEM((W,), F32),
            pltpu.VMEM((W,), F32),
            pltpu.VMEM((WIDTH,), F32),
            pltpu.VMEM((WIDTH,), F32),
            pltpu.VMEM((TOK,), jnp.int32),
            pltpu.VMEM((2, 2, 3 * TOK, W), BF),
            pltpu.VMEM((2, TOK, W), BF),
            pltpu.VMEM((TOK, W), BF),
            pltpu.VMEM((2, 8, 48, W), BF),
            pltpu.VMEM((2, 2, 2, 48, W), BF),
            pltpu.VMEM((2, 2, 4, 48, W), BF),
            pltpu.VMEM((2, 3, 16, W), BF),
            pltpu.VMEM((2, 4, 16, W), BF),
            pltpu.VMEM((8, 48, W), BF),
            pltpu.VMEM((8, 48, W), BF),
            pltpu.VMEM((8, 32, W), BF),
            pltpu.VMEM((8, 32, W), BF),
            pltpu.VMEM((8, TOK), F32),
            pltpu.VMEM((8, 8, TOK), F32),
            pltpu.VMEM((8, TOK), F32),
            pltpu.VMEM((8, TOK), F32),
            pltpu.VMEM((8, TOK), F32),
            pltpu.VMEM((8, 8, TOK), F32),
            pltpu.VMEM((4, 8, TOK), F32),
            pltpu.VMEM((8, TOK), F32),
            pltpu.VMEM((8, 32, W), BF),
            pltpu.VMEM((8, 32, W), BF),
            dma((13,)),
            dma((280,)),
            dma((8,)),
            dma((1,)),
            dma((8,)),
            dma((4,)),
            dma((8,)),
            dma((8,)),
            dma((3, 8)),
            dma((2, 2, 2)),
            dma((2, 2, 4, 3)),
            dma((2, 4)),
            dma((2, 3)),
            dma((2, 2, 4, 3)),
            dma((2, 8, 3)),
        ],
        compiler_params=pltpu.CompilerParams(
            collective_id=0, has_side_effects=True, vmem_limit_bytes=56 * 1024 * 1024
        ),
    )(
        keyframes,
        switch_step,
        q_high,
        k_high,
        v_high,
        gain_qh,
        gain_kh,
        q_low,
        k_low,
        v_low,
        gain_ql,
        gain_kl,
        permutation,
    )


def solution(mesh):
    return jax.shard_map(
        body,
        mesh=mesh,
        in_specs=(
            P("frame", "head"),
            P("frame", "head"),
            P("frame", "head"),
            P("head"),
            P("head"),
            P(("frame", "head"), None),
            P(("frame", "head"), None),
            P(("frame", "head"), None),
            P(),
            P(),
            P(),
            P(),
            P(),
        ),
        out_specs=P(("frame", "head"), None),
        check_vma=False,
    )
```
